256 devices in a mesh: bucket: 16 (over z, core), replica: 16 (over y, x).
Axes of the slice: x: 4, y: 4, z: 8, core: 2. Of those that a mesh axis runs over, the one named last changes fastest.
Arguments:
- rows: bfloat16 [262144, 768], P(('bucket', 'replica')), may hold values from -40 to 40, as said below
- cell_ids: int32 [262144, 1], P(('bucket', 'replica')), may hold values from 0 to 15; in each aligned block of 1024 rows (0 to 1023, 1024 to 2047, ...) at most 128 rows name the same one
- start_basis: float32 [16, 768, 768], P('bucket'), may hold values from -0.1 to 1.1, as said below
Outputs:
- rotated: bfloat16 [262144, 768], P(('bucket', 'replica'))
The draws below stay inside these ranges and needn't reach their ends.
Inputs may be any that keep to these rules, and one draw needn't show every extreme that they name: `cell_ids`: in the rows of one device no cell is named by more than 128 rows, a bound that some block reaches; every cell is named by some row. `rows`: A residual row: a column offset plus rough noise with column and row scales. `start_basis`: the identity plus small dense entries.
All inputs are finite; a program needn't handle non-finite values.
Results may differ from the reference program's by a relative error of at most 0.0049.
Values may be sent and summed in bfloat16 or wider, within the bound.
A program may use at most 128 MiB of HBM per device.

```python
import math
import jax
import jax.numpy as jnp
import numpy as np
from jax import lax

D = 768
CELLS = 16
ROWS_DEV = 1024
ITERS_NS = 3
CAP = 128
ROWS = 262144


def draw_rows(key, part):
    keys = jax.random.split(key, 4)
    column_scale = jnp.exp(jax.random.uniform(keys[0], (1, D), jnp.float32, 0.0, math.log(4.0)))
    offset = jax.random.uniform(keys[1], (1, D), jnp.float32, -1.0, 1.0)
    row_scale = jnp.exp(jax.random.uniform(keys[2], (ROWS, 1), jnp.float32, math.log(0.3), math.log(3.0)))
    noise = jax.random.normal(keys[3], (ROWS, D), jnp.float32)
    values = jnp.clip(offset + noise * column_scale * row_scale, -40.0, 40.0)
    return values.astype(jnp.bfloat16)


def draw_start_basis(key, part):
    noise = jnp.clip(jax.random.normal(key, (CELLS, D, D), jnp.float32) * (0.5 / math.sqrt(D)), -0.1, 0.1)
    return jnp.eye(D, dtype=jnp.float32)[None, :, :] + noise


def assign_block(rng, own, number, rows, amount, top, bound, skew):
    order = jax.random.permutation(rng, amount)
    crowded, common = shares(amount, rows * top, bound, skew, True), shares(amount, rows * top, bound, skew, False)
    places = jnp.arange(amount)

    def named(lengths, offset_by):
        used = int((lengths > 0).sum())
        fixed = max(1, used // 4)
        shifted = fixed + (places - fixed + offset_by * (used - fixed)) % max(1, amount - fixed)
        return jnp.zeros((amount,), jnp.int32).at[order[jnp.where(places < fixed, places, shifted)]].set(jnp.asarray(lengths, jnp.int32))

    lengths = jnp.where(number % 4 == 0, named(crowded, number // 4), named(common, number - number // 4 - 1))
    mixed = jax.random.permutation(jax.random.fold_in(own, 3), amount)
    source_of, receiver = mixed[0:amount // 2 * 2:2], mixed[1:amount // 2 * 2:2]
    slack = jnp.minimum(lengths[source_of] - 1, bound - lengths[receiver]) // 2
    slack = jnp.where((source_of == order[0]) | (receiver == order[0]) | (lengths[receiver] == 0), 0, jnp.maximum(slack, 0))
    shifted = jax.random.randint(jax.random.fold_in(own, 4), (amount // 2,), 0, 1 << 20) % (slack + 1)
    lengths = lengths.at[source_of].add(-shifted).at[receiver].add(shifted)
    labels = jnp.searchsorted(jnp.cumsum(lengths), jnp.arange(rows * top), side="right").astype(jnp.int32)
    listing = labels.reshape(top, rows).T
    listing = listing[jax.random.permutation(jax.random.fold_in(own, 1), rows)]
    offset_by = jax.random.randint(jax.random.fold_in(own, 2), (rows, 1), 0, top)
    return jnp.take_along_axis(listing, (jnp.arange(top)[None, :] + offset_by) % top, axis=1)


def shares(number_of, total, limit, slope, full):
    portions = [(1 << 20) // math.isqrt(standing ** slope) + 1 for standing in range(1, number_of + 1)]
    largest = limit if full else min(limit, max(-(-total // number_of), total * portions[0] // sum(portions)))
    least = 1 if total - largest >= number_of - 1 else 0
    given, rest = [largest] + [least] * (number_of - 1), total - largest - least * (number_of - 1)
    while rest > 0:
        movable = [i for i in range(1, number_of) if given[i] < largest] or [i for i in range(1, number_of) if given[i] < limit]
        whole, budget = sum([portions[i] for i in movable]), rest
        for i in movable:
            extra = min(limit - given[i], max(1, budget * portions[i] // whole), rest)
            given[i] = given[i] + extra
            rest = rest - extra
    return np.array(given)


def setup_inputs(seed: int = 0) -> dict:
    arg_keys = jax.random.split(jax.random.key(seed), 4)
    rows = draw_rows(jax.random.fold_in(arg_keys[3], 71), 0)
    cell_ids_keys = jax.random.split(jax.random.fold_in(arg_keys[1], 1), ROWS // ROWS_DEV)
    cell_ids_turns = jax.random.permutation(jax.random.fold_in(arg_keys[1], 3), ROWS // ROWS_DEV)
    cell_ids = jax.vmap(lambda own, number: assign_block(jax.random.fold_in(arg_keys[1], 2), own, number, ROWS_DEV, CELLS, 1, CAP, 0))(cell_ids_keys, cell_ids_turns).reshape((ROWS, 1))
    start_basis = draw_start_basis(jax.random.fold_in(arg_keys[3], 71), 0)
    return dict(rows=rows, cell_ids=cell_ids, start_basis=start_basis)


def orthogonalise(count, total, square, basis):
    mean = total / jnp.maximum(count, 1.0)
    covariance = square / jnp.maximum(count, 1.0) - mean[:, None] * mean[None, :]
    current = basis
    for step in range(ITERS_NS):
        image = jnp.dot(covariance, current, precision=lax.Precision.HIGHEST)
        gram_matrix = jnp.dot(image.T, image, precision=lax.Precision.HIGHEST)
        factor = jnp.linalg.cholesky(gram_matrix)
        current = jax.scipy.linalg.solve_triangular(factor, image.T, lower=True).T
    rotation = current.astype(jnp.bfloat16)
    shift = jnp.dot(mean, rotation.astype(jnp.float32), precision=lax.Precision.HIGHEST)
    return (rotation, shift)

def reference(rows, cell_ids, start_basis):
    total_rows = rows.shape[0]
    width = rows.shape[1]
    flat_ids = cell_ids[:, 0].astype(jnp.int32)
    order = jnp.argsort(flat_ids, stable=True).astype(jnp.int32)
    onehot = (flat_ids[:, None] == jnp.arange(CELLS, dtype=jnp.int32)[None, :]).astype(jnp.int32)
    counts = jnp.sum(onehot, axis=0).astype(jnp.int32)
    starts = (jnp.cumsum(counts) - counts).astype(jnp.int32)
    block = 1024
    sorted_rows = jnp.concatenate([rows[order], jnp.zeros((block, width), rows.dtype)], axis=0)
    positions = jnp.arange(block, dtype=jnp.int32)

    def block_range(cell):
        first = starts[cell]
        last = first + counts[cell]
        return (first, last, (first // block).astype(jnp.int32), ((last + block - 1) // block).astype(jnp.int32))

    def moments(cell):
        first, last, lower, upper = block_range(cell)

        def add_block(index, carry):
            total, square = carry
            begin = (index * block).astype(jnp.int32)
            piece = lax.dynamic_slice_in_dim(sorted_rows, begin, block, 0)
            keep = (begin + positions >= first) & (begin + positions < last)
            piece = jnp.where(keep[:, None], piece, jnp.zeros_like(piece))
            total = total + jnp.sum(piece, axis=0, dtype=jnp.float32)
            square = square + jnp.dot(piece.T.astype(jnp.float32), piece.astype(jnp.float32), preferred_element_type=jnp.float32)
            return (total, square)
        start_carry = (jnp.zeros((width,), jnp.float32), jnp.zeros((width, width), jnp.float32))
        return lax.fori_loop(lower, upper, add_block, start_carry)
    totals, squares = lax.map(moments, jnp.arange(CELLS, dtype=jnp.int32))

    def one_cell(packed):
        return orthogonalise(packed[0], packed[1], packed[2], packed[3])
    rotations, shifts = lax.map(one_cell, (counts.astype(jnp.float32), totals, squares, start_basis))

    def rotate_cell(cell, sorted_out):
        first, last, lower, upper = block_range(cell)
        rotation = rotations[cell]
        shift = shifts[cell]

        def write_block(index, buffer):
            begin = (index * block).astype(jnp.int32)
            piece = lax.dynamic_slice_in_dim(sorted_rows, begin, block, 0)
            value = (jnp.dot(piece.astype(jnp.float32), rotation.astype(jnp.float32), preferred_element_type=jnp.float32) - shift[None, :]).astype(jnp.bfloat16)
            keep = (begin + positions >= first) & (begin + positions < last)
            previous = lax.dynamic_slice_in_dim(buffer, begin, block, 0)
            return lax.dynamic_update_slice_in_dim(buffer, jnp.where(keep[:, None], value, previous), begin, 0)
        return lax.fori_loop(lower, upper, write_block, sorted_out)
    sorted_out = lax.fori_loop(0, CELLS, rotate_cell, jnp.zeros((total_rows + block, width), jnp.bfloat16))
    return jnp.zeros((total_rows, width), jnp.bfloat16).at[order].set(sorted_out[:total_rows])
```

```python
import functools

import jax
import jax.numpy as jnp
from jax import lax
from jax.experimental import pallas as pl
from jax.experimental.pallas import tpu as pltpu
from jax.sharding import PartitionSpec as P

CELLS = 16
SWEEPS = 3
CAP = 128
D = 768
RB = 128
NB = D // RB
ROWS = 1024
SLOTS = CELLS * CAP
F32 = jnp.float32
BF16 = jnp.bfloat16
NT = (((1,), (1,)), ((), ()))
TN = (((0,), (0,)), ((), ()))
VMEM = pl.BlockSpec(memory_space=pltpu.VMEM)


def params(mib, **kw):
    return pltpu.CompilerParams(vmem_limit_bytes=mib * 2**20, **kw)


def dot(a, b):
    return jnp.dot(a, b, preferred_element_type=F32)


def dot_nt(a, b):
    return lax.dot_general(a, b, NT, preferred_element_type=F32)


def halves(x):
    high = x.astype(BF16)
    return high, (x - high.astype(F32)).astype(BF16)


def dispatch_kernel(ids_ref, rows_ref, buffer_ref, counts_ref, place_ref):
    ids = ids_ref[...]
    cells = lax.broadcasted_iota(jnp.int32, (CELLS, ROWS), 0)
    onehot = (ids == cells).astype(F32)
    before = (
        lax.broadcasted_iota(jnp.int32, (ROWS, ROWS), 0)
        < lax.broadcasted_iota(jnp.int32, (ROWS, ROWS), 1)
    ).astype(F32).astype(BF16)
    ranks = dot(onehot.astype(BF16), before)
    slot = jnp.sum(ranks * onehot, axis=0, keepdims=True).astype(jnp.int32)
    place = ids * CAP + slot
    counts_ref[...] = jnp.broadcast_to(jnp.sum(onehot, axis=1, keepdims=True), (CELLS, 128))
    place_ref[...] = jnp.broadcast_to(place, (128, ROWS)).T

    def fill(cell, carry):
        wanted = lax.broadcasted_iota(jnp.int32, (CAP, ROWS), 0) + cell * CAP
        pick = (place == wanted).astype(F32).astype(BF16)
        first = pl.multiple_of(cell * CAP, CAP)
        buffer_ref[pl.ds(first, CAP), :] = dot(pick, rows_ref[...]).astype(BF16)
        return carry

    lax.fori_loop(0, CELLS, fill, 0)


def moments_kernel(received_ref, counts_ref, out_ref):
    for block in range(D // 256):
        columns = pl.ds(block * 256, 256)
        out_ref[columns, :] = lax.dot_general(
            received_ref[:, columns], received_ref[...], TN, preferred_element_type=F32
        )
    ones = jnp.ones((8, SLOTS), BF16)
    total = dot(ones, received_ref[...])
    count = jnp.sum(counts_ref[...])
    is_total = lax.broadcasted_iota(jnp.int32, (8, D), 0) == 0
    out_ref[D : D + 8, :] = jnp.where(is_total, total, count)


def factor(a_ref, m_ref):
    n = RB // 8
    shape = (8, RB)
    sub = lax.broadcasted_iota(jnp.int32, shape, 0)
    lane = lax.broadcasted_iota(jnp.int32, shape, 1)
    a = [a_ref[8 * r : 8 * r + 8, :] for r in range(n)]
    m = [(lane == sub + 8 * r).astype(F32) for r in range(n)]
    for b in range(n):
        col = [
            [jnp.broadcast_to(a[r][:, 8 * b + j : 8 * b + j + 1], shape) for j in range(8)]
            if r >= b
            else None
            for r in range(n)
        ]
        s = [
            [jnp.broadcast_to(col[b][j][i : i + 1, :], shape) if i >= j else None for j in range(8)]
            for i in range(8)
        ]
        t = [[None] * 8 for _ in range(8)]
        inverse = [None] * 8
        for j in range(8):
            inverse[j] = 1.0 / s[j][j]
            for i in range(j + 1, 8):
                t[i][j] = s[i][j] * inverse[j]
            for k in range(j + 1, 8):
                for i in range(k, 8):
                    s[i][k] = s[i][k] - t[k][j] * s[i][j]
        low = [[None] * 8 for _ in range(n)]
        for r in range(b, n):
            for j in range(8):
                for i in range(j + 1, 8):
                    col[r][i] = col[r][i] - col[r][j] * t[i][j]
                low[r][j] = col[r][j] * inverse[j]
        panel, inv_panel = a[b], m[b]
        rows, inv_rows = [], []
        for j in range(8):
            rows.append(jnp.broadcast_to(panel[j : j + 1, :], shape))
            inv_rows.append(jnp.broadcast_to(inv_panel[j : j + 1, :], shape))
            if j < 7:
                below = jnp.where(sub > j, low[b][j], 0.0)
                panel = panel - below * rows[j]
                inv_panel = inv_panel - below * inv_rows[j]
        pivots = s[0][0]
        for j in range(1, 8):
            pivots = jnp.where(sub == j, s[j][j], pivots)
        m[b] = inv_panel * lax.rsqrt(pivots)
        for r in range(b + 1, n):
            for j in range(8):
                a[r] = a[r] - low[r][j] * rows[j]
                m[r] = m[r] - low[r][j] * inv_rows[j]
    for r in range(n):
        m_ref[8 * r : 8 * r + 8, :] = m[r]


def sweeps_kernel(
    reduced_ref, start_ref, w_high, shift_ref, c_high, c_low, y, y_high, y_low, w_low, gram, inverse
):
    tail = reduced_ref[D : D + 8, :]
    divisor = jnp.maximum(tail[1:2, :], 1.0)
    mean = tail[0:1, :] / divisor
    first = lax.broadcasted_iota(jnp.int32, (8, D), 0) == 0
    mean_rows = jnp.where(first, jnp.broadcast_to(mean, (8, D)), 0.0)
    for block in range(NB):
        span = slice(block * RB, block * RB + RB)
        outer = lax.dot_general(
            mean_rows[:, span], mean_rows, TN, preferred_element_type=F32,
            precision=lax.Precision.HIGHEST,
        )
        high, low = halves(reduced_ref[span, :] / divisor - outer)
        c_high[span, :] = high
        c_low[span, :] = low
        high, low = halves(start_ref[:, span].T)
        w_high[span, :] = high
        w_low[span, :] = low

    def sweep(step, carry):
        for block in range(D // 256):
            span = slice(block * 256, block * 256 + 256)
            image = (
                dot(w_high[span, :], c_high[...])
                + dot(w_high[span, :], c_low[...])
                + dot(w_low[span, :], c_high[...])
            )
            y[span, :] = image
            high, low = halves(image)
            y_high[span, :] = high
            y_low[span, :] = low

        def block_step(block, inner):
            span = pl.ds(pl.multiple_of(block * RB, RB), RB)
            high, low = y_high[span, :], y_low[span, :]
            gram[...] = dot_nt(high, high) + dot_nt(high, low) + dot_nt(low, high)
            factor(gram, inverse)
            i_high, i_low = halves(inverse[...])
            w_h, w_l = halves(dot(i_high, high) + dot(i_high, low) + dot(i_low, high))
            w_high[span, :] = w_h
            w_low[span, :] = w_l
            for done in range(NB - 1):

                @pl.when(block == done)
                def _():
                    rest = slice(RB * (done + 1), D)
                    own = slice(RB * done, RB * done + RB)
                    u_h, u_l = w_high[own, :], w_low[own, :]
                    r_h, r_l = y_high[rest, :], y_low[rest, :]
                    l_h, l_l = halves(dot_nt(r_h, u_h) + dot_nt(r_h, u_l) + dot_nt(r_l, u_h))
                    left = y[rest, :] - (dot(l_h, u_h) + dot(l_h, u_l) + dot(l_l, u_h))
                    y[rest, :] = left
                    high, low = halves(left)
                    y_high[rest, :] = high
                    y_low[rest, :] = low

            return inner

        return lax.fori_loop(0, NB, block_step, carry)

    lax.fori_loop(0, SWEEPS, sweep, 0)
    shift_ref[...] = lax.dot_general(
        jnp.broadcast_to(mean, (8, D)), w_high[...].astype(F32), NT,
        preferred_element_type=F32, precision=lax.Precision.HIGHEST,
    )


def rotate_kernel(received_ref, w_ref, shift_ref, out_ref):
    def step(index, carry):
        span = pl.ds(pl.multiple_of(index * 256, 256), 256)
        product = dot_nt(received_ref[span, :], w_ref[...])
        out_ref[span, :] = (product - shift_ref[0:1, :]).astype(BF16)
        return carry

    lax.fori_loop(0, SLOTS // 256, step, 0)


def collect_kernel(returned_ref, place_ref, out_ref):
    def step(index, carry):
        span = pl.ds(pl.multiple_of(index * 256, 256), 256)
        place = place_ref[span, :]
        lane = lax.broadcasted_iota(jnp.int32, (256, CAP), 1)
        pick = jnp.concatenate(
            [(place == lane + cell * CAP).astype(F32).astype(BF16) for cell in range(CELLS)], axis=1
        )
        out_ref[span, :] = dot(pick, returned_ref[...]).astype(BF16)
        return carry

    lax.fori_loop(0, ROWS // 256, step, 0)


def sweeps(reduced, start):
    return pl.pallas_call(
        sweeps_kernel,
        out_shape=[jax.ShapeDtypeStruct((D, D), BF16), jax.ShapeDtypeStruct((8, D), F32)],
        in_specs=[VMEM, VMEM],
        out_specs=[VMEM, VMEM],
        scratch_shapes=[
            pltpu.VMEM((D, D), BF16),
            pltpu.VMEM((D, D), BF16),
            pltpu.VMEM((D, D), F32),
            pltpu.VMEM((D, D), BF16),
            pltpu.VMEM((D, D), BF16),
            pltpu.VMEM((D, D), BF16),
            pltpu.VMEM((RB, RB), F32),
            pltpu.VMEM((RB, RB), F32),
        ],
        compiler_params=params(48),
        name="sweeps",
    )(reduced, start)


def body(rows, cell_ids, start_basis):
    buffer, counts, place = pl.pallas_call(
        dispatch_kernel,
        out_shape=[
            jax.ShapeDtypeStruct((SLOTS, D), BF16),
            jax.ShapeDtypeStruct((CELLS, 128), F32),
            jax.ShapeDtypeStruct((ROWS, 128), jnp.int32),
        ],
        in_specs=[VMEM, VMEM],
        out_specs=[VMEM] * 3,
        compiler_params=params(40),
        name="dispatch",
    )(cell_ids.reshape(1, ROWS), rows)
    received = lax.all_to_all(buffer, "bucket", split_axis=0, concat_axis=0, tiled=True)
    recv_counts = lax.all_to_all(counts[:, :1], "bucket", split_axis=0, concat_axis=0, tiled=True)
    partial = pl.pallas_call(
        moments_kernel,
        out_shape=jax.ShapeDtypeStruct((D + 8, D), F32),
        in_specs=[VMEM, VMEM],
        out_specs=VMEM,
        compiler_params=params(40),
        name="moments",
    )(received, recv_counts)
    reduced = lax.psum(partial, "replica")
    rotation, shift = sweeps(reduced, start_basis[0])
    rotated = pl.pallas_call(
        rotate_kernel,
        out_shape=jax.ShapeDtypeStruct((SLOTS, D), BF16),
        in_specs=[VMEM] * 3,
        out_specs=VMEM,
        compiler_params=params(40),
        name="rotate",
    )(received, rotation, shift)
    returned = lax.all_to_all(rotated, "bucket", split_axis=0, concat_axis=0, tiled=True)
    return pl.pallas_call(
        collect_kernel,
        out_shape=jax.ShapeDtypeStruct((ROWS, D), BF16),
        in_specs=[VMEM] * 2,
        out_specs=VMEM,
        compiler_params=params(40),
        name="collect",
    )(returned, place)


def solution(mesh):
    both = P(("bucket", "replica"), None)
    return jax.shard_map(
        body,
        mesh=mesh,
        in_specs=(both, both, P("bucket", None, None)),
        out_specs=both,
        check_vma=False,
    )
```

```python
import functools

import jax
import jax.numpy as jnp
from jax import lax
from jax.experimental import pallas as pl
from jax.experimental.pallas import tpu as pltpu
from jax.sharding import PartitionSpec as P

CELLS = 16
SWEEPS = 3
CAP = 128
D = 768
RB = 128
NB = D // RB
ROWS = 1024
SLOTS = CELLS * CAP
F32 = jnp.float32
BF16 = jnp.bfloat16
NT = (((1,), (1,)), ((), ()))
TN = (((0,), (0,)), ((), ()))
VMEM = pl.BlockSpec(memory_space=pltpu.VMEM)
ANY = pl.BlockSpec(memory_space=pl.ANY)
MESH = pl.DeviceIdType.MESH
DMA = pltpu.SemaphoreType.DMA
PLANE = 16
RING = 8
PAIRS = [(i, j) for i in range(NB) for j in range(i, NB)]
CHUNK = 176
HALF = RING * CHUNK
PACKED = 2 * HALF
TAIL = len(PAIRS) * RB
PIECES = 12
PIECE = D // PIECES


def params(mib, **kw):
    return pltpu.CompilerParams(vmem_limit_bytes=mib * 2**20, **kw)


def dot(a, b):
    return jnp.dot(a, b, preferred_element_type=F32)


def dot_nt(a, b):
    return lax.dot_general(a, b, NT, preferred_element_type=F32)


def halves(x):
    high = x.astype(BF16)
    return high, (x - high.astype(F32)).astype(BF16)


def dispatch_kernel(ids_ref, rows_ref, buffer_ref, counts_ref, place_ref):
    ids = ids_ref[...]
    cells = lax.broadcasted_iota(jnp.int32, (CELLS, ROWS), 0)
    onehot = (ids == cells).astype(F32)
    before = (
        lax.broadcasted_iota(jnp.int32, (ROWS, ROWS), 0)
        < lax.broadcasted_iota(jnp.int32, (ROWS, ROWS), 1)
    ).astype(F32).astype(BF16)
    ranks = dot(onehot.astype(BF16), before)
    slot = jnp.sum(ranks * onehot, axis=0, keepdims=True).astype(jnp.int32)
    place = ids * CAP + slot
    eighth = lax.broadcasted_iota(jnp.int32, (8 * CELLS, ROWS), 0) // 8
    each = jnp.sum((ids == eighth).astype(F32), axis=1, keepdims=True)
    counts_ref[...] = jnp.broadcast_to(each, (8 * CELLS, 128))
    place_ref[...] = jnp.broadcast_to(place, (128, ROWS)).T

    def fill(cell, carry):
        wanted = lax.broadcasted_iota(jnp.int32, (CAP, ROWS), 0) + cell * CAP
        pick = (place == wanted).astype(F32).astype(BF16)
        first = pl.multiple_of(cell * CAP, CAP)
        buffer_ref[pl.ds(first, CAP), :] = dot(pick, rows_ref[...]).astype(BF16)
        return carry

    lax.fori_loop(0, CELLS, fill, 0)


def scatter_kernel(
    buffer_ref, counts_ref, basis_ref, received_ref, got_counts_ref, got_basis_ref,
    send, recv, send_count, recv_count, send_up, send_down, send_across, recv_chain, recv_across, own
):
    bucket, me = lax.axis_index("bucket"), lax.axis_index("replica")
    z, core = bucket // 2, bucket % 2
    origin, chain_core = me // 2, me % 2
    away = lax.rem(z + RING - origin, RING)
    up = lax.rem(z + 1, RING) * 2 + core
    down = lax.rem(z + RING - 1, RING) * 2 + core
    across = z * 2 + (1 - core)
    peers = plane_peers(me)

    barrier = pltpu.get_barrier_semaphore()
    for peer in peers:
        pl.semaphore_signal(barrier, inc=1, device_id=(bucket, peer), device_id_type=MESH)
    for other in (up, down, across):
        pl.semaphore_signal(barrier, inc=1, device_id=(other, me), device_id_type=MESH)
    pl.semaphore_wait(barrier, len(peers) + 3)

    copies = []
    for index, peer in enumerate(peers):
        copies.append(pltpu.make_async_remote_copy(
            counts_ref.at[pl.ds(pl.multiple_of(peer * 8, 8), 8)],
            got_counts_ref.at[pl.ds(pl.multiple_of(me * 8, 8), 8)],
            send_count.at[index], recv_count.at[index], device_id=(bucket, peer), device_id_type=MESH,
        ))
        copies.append(exchange(buffer_ref, received_ref, send, recv, index, bucket, me, peer))
    for copy in copies:
        copy.start()
    mine = pl.ds(pl.multiple_of(me * CAP, CAP), CAP)
    mine_counts = pl.ds(pl.multiple_of(me * 8, 8), 8)
    local = [
        pltpu.make_async_copy(buffer_ref.at[mine], received_ref.at[mine], own.at[0]),
        pltpu.make_async_copy(counts_ref.at[mine_counts], got_counts_ref.at[mine_counts], own.at[1]),
    ]
    for copy in local:
        copy.start()

    def passing(source, index, sends, receives, target):
        span = pl.ds(index * PIECE, PIECE)
        return pltpu.make_async_remote_copy(
            source.at[span], got_basis_ref.at[span], sends.at[index], receives.at[index],
            device_id=(target, me), device_id_type=MESH,
        )

    on_chain = core == chain_core
    first = on_chain & (away == 0)
    later = on_chain & (away > 0)

    @pl.when(first)
    def _():
        whole = pltpu.make_async_copy(basis_ref, got_basis_ref, own.at[2])
        whole.start()
        for index in range(PIECES):
            passing(basis_ref, index, send_up, recv_chain, up).start()
            passing(basis_ref, index, send_down, recv_chain, down).start()
            passing(basis_ref, index, send_across, recv_across, across).start()
        for index in range(PIECES):
            passing(basis_ref, index, send_up, recv_chain, up).wait_send()
            passing(basis_ref, index, send_down, recv_chain, down).wait_send()
            passing(basis_ref, index, send_across, recv_across, across).wait_send()
        whole.wait()

    @pl.when(later)
    def _():
        upward = away < 4
        downward = away > 5
        for index in range(PIECES):
            passing(got_basis_ref, index, send_up, recv_chain, up).wait_recv()

            @pl.when(upward)
            def _():
                passing(got_basis_ref, index, send_up, recv_chain, up).start()

            @pl.when(downward)
            def _():
                passing(got_basis_ref, index, send_down, recv_chain, down).start()

            passing(got_basis_ref, index, send_across, recv_across, across).start()
        for index in range(PIECES):
            @pl.when(upward)
            def _():
                passing(got_basis_ref, index, send_up, recv_chain, up).wait_send()

            @pl.when(downward)
            def _():
                passing(got_basis_ref, index, send_down, recv_chain, down).wait_send()

            passing(got_basis_ref, index, send_across, recv_across, across).wait_send()

    @pl.when(core != chain_core)
    def _():
        for index in range(PIECES):
            passing(got_basis_ref, index, send_across, recv_across, across).wait_recv()

    for copy in copies + local:
        copy.wait()


def plane_peers(me):
    y, x = me // 4, me % 4
    return [
        lax.rem(y + dy, 4) * 4 + lax.rem(x + dx, 4)
        for dy, dx in sorted(
            ((dy, dx) for dy in range(4) for dx in range(4) if dy or dx),
            key=lambda o: -min(o[0], 4 - o[0]) - min(o[1], 4 - o[1]),
        )
    ]


def exchange(source, target, send, recv, index, bucket, me, peer):
    return pltpu.make_async_remote_copy(
        source.at[pl.ds(pl.multiple_of(peer * CAP, CAP), CAP)],
        target.at[pl.ds(pl.multiple_of(me * CAP, CAP), CAP)],
        send.at[index], recv.at[index], device_id=(bucket, peer), device_id_type=MESH,
    )


def giveback_kernel(rotated_ref, returned_ref, send, recv, own):
    bucket, me = lax.axis_index("bucket"), lax.axis_index("replica")
    peers = plane_peers(me)
    barrier = pltpu.get_barrier_semaphore()
    for peer in peers:
        pl.semaphore_signal(barrier, inc=1, device_id=(bucket, peer), device_id_type=MESH)
    pl.semaphore_wait(barrier, len(peers))
    copies = [
        exchange(rotated_ref, returned_ref, send, recv, index, bucket, me, peer)
        for index, peer in enumerate(peers)
    ]
    mine = pl.ds(pl.multiple_of(me * CAP, CAP), CAP)
    copies.append(pltpu.make_async_copy(rotated_ref.at[mine], returned_ref.at[mine], own.at[0]))
    for copy in copies:
        copy.start()
    for copy in copies:
        copy.wait()


def moments_kernel(received_ref, counts_ref, out_ref):
    place = 0
    for block in range(NB):
        rest = slice(block * RB, D)
        square = lax.dot_general(
            received_ref[:, block * RB : block * RB + RB], received_ref[:, rest], TN,
            preferred_element_type=F32,
        )
        for other in range(NB - block):
            out_ref[place : place + RB, :] = square[:, other * RB : other * RB + RB]
            place += RB
    total = dot(jnp.ones((8, SLOTS), BF16), received_ref[...])
    out_ref[TAIL:PACKED, :] = jnp.zeros((PACKED - TAIL, RB), F32)
    for block in range(NB):
        out_ref[TAIL + block : TAIL + block + 1, :] = total[0:1, block * RB : block * RB + RB]
    count = jnp.sum(counts_ref[...].reshape(CELLS, 8, 128)[:, 0, :], axis=0, keepdims=True)
    out_ref[TAIL + NB : TAIL + NB + 1, :] = count


def reduce_kernel(
    part_ref, out_ref, full, arrived, mine, slots, send_half, recv_half, send_part, recv_part,
    send_all, recv_all, send_across, recv_across
):
    bucket, me = lax.axis_index("bucket"), lax.axis_index("replica")
    z, core = bucket // 2, bucket % 2
    across = (z * 2 + (1 - core), me)
    ring = [(lax.rem(z + step, RING) * 2 + core, me) for step in range(RING)]
    barrier = pltpu.get_barrier_semaphore()
    for other in [across] + ring[1:]:
        pl.semaphore_signal(barrier, inc=1, device_id=other, device_id_type=MESH)
    pl.semaphore_wait(barrier, RING)

    half = pltpu.make_async_remote_copy(
        part_ref.at[pl.ds(pl.multiple_of((1 - core) * HALF, 8), HALF)], arrived,
        send_half, recv_half, device_id=across, device_id_type=MESH,
    )
    half.start()
    half.wait()
    mine[...] = part_ref[pl.ds(pl.multiple_of(core * HALF, 8), HALF), :] + arrived[...]

    order = [4, 3, 5, 2, 6, 1, 7]
    parts = []
    for step in order:
        chunk = lax.rem(z + step, RING)
        parts.append(pltpu.make_async_remote_copy(
            mine.at[pl.ds(pl.multiple_of(chunk * CHUNK, 8), CHUNK)], slots.at[step],
            send_part.at[step], recv_part.at[step], device_id=ring[step], device_id_type=MESH,
        ))
    for copy in parts:
        copy.start()
    total = mine[pl.ds(pl.multiple_of(z * CHUNK, 8), CHUNK), :]
    for step, copy in zip(order, parts):
        copy.wait_recv()
        total = total + slots[step]

    def chunk_of(where):
        return pl.ds(pl.multiple_of((core * RING + where) * CHUNK, 8), CHUNK)

    full[chunk_of(z), :] = total
    spread = [
        pltpu.make_async_remote_copy(
            full.at[chunk_of(z)], full.at[chunk_of(z)], send_all.at[step], recv_all.at[step],
            device_id=ring[step], device_id_type=MESH,
        )
        for step in order
    ]
    for copy in spread:
        copy.start()

    def forward(step):
        where = chunk_of(lax.rem(z + RING - step, RING))
        return pltpu.make_async_remote_copy(
            full.at[where], full.at[where], send_across.at[step], recv_across.at[step],
            device_id=across, device_id_type=MESH,
        )

    forward(0).start()
    for step, copy in sorted(zip(order, spread), key=lambda item: min(item[0], RING - item[0])):
        copy.wait_recv()
        forward(step).start()
    for step in range(RING):
        forward(step).wait()
    for copy in parts + spread:
        copy.wait_send()
    out_ref[...] = full[...]


def factor(a_ref, m_ref):
    n = RB // 8
    shape = (8, RB)
    sub = lax.broadcasted_iota(jnp.int32, shape, 0)
    lane = lax.broadcasted_iota(jnp.int32, shape, 1)
    a = [a_ref[8 * r : 8 * r + 8, :] for r in range(n)]
    m = [(lane == sub + 8 * r).astype(F32) for r in range(n)]
    for b in range(n):
        col = [
            [jnp.broadcast_to(a[r][:, 8 * b + j : 8 * b + j + 1], shape) for j in range(8)]
            if r >= b
            else None
            for r in range(n)
        ]
        s = [
            [jnp.broadcast_to(col[b][j][i : i + 1, :], shape) if i >= j else None for j in range(8)]
            for i in range(8)
        ]
        t = [[None] * 8 for _ in range(8)]
        inverse = [None] * 8
        for j in range(8):
            inverse[j] = 1.0 / s[j][j]
            for i in range(j + 1, 8):
                t[i][j] = s[i][j] * inverse[j]
            for k in range(j + 1, 8):
                for i in range(k, 8):
                    s[i][k] = s[i][k] - t[k][j] * s[i][j]
        low = [[None] * 8 for _ in range(n)]
        for r in range(b, n):
            for j in range(8):
                for i in range(j + 1, 8):
                    col[r][i] = col[r][i] - col[r][j] * t[i][j]
                low[r][j] = col[r][j] * inverse[j]
        panel, inv_panel = a[b], m[b]
        rows, inv_rows = [], []
        for j in range(8):
            rows.append(jnp.broadcast_to(panel[j : j + 1, :], shape))
            inv_rows.append(jnp.broadcast_to(inv_panel[j : j + 1, :], shape))
            if j < 7:
                below = jnp.where(sub > j, low[b][j], 0.0)
                panel = panel - below * rows[j]
                inv_panel = inv_panel - below * inv_rows[j]
        pivots = s[0][0]
        for j in range(1, 8):
            pivots = jnp.where(sub == j, s[j][j], pivots)
        m[b] = inv_panel * lax.rsqrt(pivots)
        for r in range(b + 1, n):
            for j in range(8):
                a[r] = a[r] - low[r][j] * rows[j]
                m[r] = m[r] - low[r][j] * inv_rows[j]
    for r in range(n):
        m_ref[8 * r : 8 * r + 8, :] = m[r]


def sweeps_kernel(
    reduced_ref, start_ref, w_high, shift_ref, c_high, c_low, y, y_high, y_low, w_low, gram, inverse
):
    count = reduced_ref[TAIL + NB : TAIL + NB + 1, :]
    divisor = jnp.maximum(count, 1.0)
    mean = jnp.concatenate(
        [reduced_ref[TAIL + block : TAIL + block + 1, :] / divisor for block in range(NB)], axis=1
    )
    first = lax.broadcasted_iota(jnp.int32, (8, D), 0) == 0
    mean_rows = jnp.where(first, jnp.broadcast_to(mean, (8, D)), 0.0)
    for block in range(NB):
        span = slice(block * RB, block * RB + RB)
        outer = lax.dot_general(
            mean_rows[:, span], mean_rows, TN, preferred_element_type=F32,
            precision=lax.Precision.HIGHEST,
        )
        for other in range(NB):
            columns = slice(other * RB, other * RB + RB)
            place = PAIRS.index((min(block, other), max(block, other))) * RB
            piece = reduced_ref[place : place + RB, :]
            if other < block:
                piece = piece.T
            high, low = halves(piece / divisor - outer[:, columns])
            c_high[span, columns] = high
            c_low[span, columns] = low
        high, low = halves(start_ref[:, span].T)
        w_high[span, :] = high
        w_low[span, :] = low

    def sweep(step, carry):
        for block in range(D // 256):
            span = slice(block * 256, block * 256 + 256)
            image = (
                dot(w_high[span, :], c_high[...])
                + dot(w_high[span, :], c_low[...])
                + dot(w_low[span, :], c_high[...])
            )
            y[span, :] = image
            high, low = halves(image)
            y_high[span, :] = high
            y_low[span, :] = low

        def block_step(block, inner):
            span = pl.ds(pl.multiple_of(block * RB, RB), RB)
            high, low = y_high[span, :], y_low[span, :]
            gram[...] = dot_nt(high, high) + dot_nt(high, low) + dot_nt(low, high)
            factor(gram, inverse)
            i_high, i_low = halves(inverse[...])
            w_h, w_l = halves(dot(i_high, high) + dot(i_high, low) + dot(i_low, high))
            w_high[span, :] = w_h
            w_low[span, :] = w_l
            for done in range(NB - 1):

                @pl.when(block == done)
                def _():
                    rest = slice(RB * (done + 1), D)
                    own = slice(RB * done, RB * done + RB)
                    u_h, u_l = w_high[own, :], w_low[own, :]
                    r_h, r_l = y_high[rest, :], y_low[rest, :]
                    l_h, l_l = halves(dot_nt(r_h, u_h) + dot_nt(r_h, u_l) + dot_nt(r_l, u_h))
                    left = y[rest, :] - (dot(l_h, u_h) + dot(l_h, u_l) + dot(l_l, u_h))
                    y[rest, :] = left
                    high, low = halves(left)
                    y_high[rest, :] = high
                    y_low[rest, :] = low

            return inner

        return lax.fori_loop(0, NB, block_step, carry)

    lax.fori_loop(0, SWEEPS, sweep, 0)
    shift_ref[...] = lax.dot_general(
        jnp.broadcast_to(mean, (8, D)), w_high[...].astype(F32), NT,
        preferred_element_type=F32, precision=lax.Precision.HIGHEST,
    )


def rotate_kernel(received_ref, w_ref, shift_ref, out_ref):
    def step(index, carry):
        span = pl.ds(pl.multiple_of(index * 256, 256), 256)
        product = dot_nt(received_ref[span, :], w_ref[...])
        out_ref[span, :] = (product - shift_ref[0:1, :]).astype(BF16)
        return carry

    lax.fori_loop(0, SLOTS // 256, step, 0)


def collect_kernel(returned_ref, place_ref, out_ref):
    def step(index, carry):
        span = pl.ds(pl.multiple_of(index * 256, 256), 256)
        place = place_ref[span, :]
        lane = lax.broadcasted_iota(jnp.int32, (256, CAP), 1)
        pick = jnp.concatenate(
            [(place == lane + cell * CAP).astype(F32).astype(BF16) for cell in range(CELLS)], axis=1
        )
        out_ref[span, :] = dot(pick, returned_ref[...]).astype(BF16)
        return carry

    lax.fori_loop(0, ROWS // 256, step, 0)


def sweeps(reduced, start):
    return pl.pallas_call(
        sweeps_kernel,
        out_shape=[jax.ShapeDtypeStruct((D, D), BF16), jax.ShapeDtypeStruct((8, D), F32)],
        in_specs=[VMEM, VMEM],
        out_specs=[VMEM, VMEM],
        scratch_shapes=[
            pltpu.VMEM((D, D), BF16),
            pltpu.VMEM((D, D), BF16),
            pltpu.VMEM((D, D), F32),
            pltpu.VMEM((D, D), BF16),
            pltpu.VMEM((D, D), BF16),
            pltpu.VMEM((D, D), BF16),
            pltpu.VMEM((RB, RB), F32),
            pltpu.VMEM((RB, RB), F32),
        ],
        compiler_params=params(48),
        name="sweeps",
    )(reduced, start)


def remote(identity):
    return params(40, collective_id=identity, has_side_effects=True)


def body(rows, cell_ids, start_basis):
    buffer, counts, place = pl.pallas_call(
        dispatch_kernel,
        out_shape=[
            jax.ShapeDtypeStruct((SLOTS, D), BF16),
            jax.ShapeDtypeStruct((8 * CELLS, 128), F32),
            jax.ShapeDtypeStruct((ROWS, 128), jnp.int32),
        ],
        in_specs=[VMEM, VMEM],
        out_specs=[VMEM] * 3,
        compiler_params=params(40),
        name="dispatch",
    )(cell_ids.reshape(1, ROWS), rows)
    received, got_counts, basis = pl.pallas_call(
        scatter_kernel,
        out_shape=[
            jax.ShapeDtypeStruct((SLOTS, D), BF16),
            jax.ShapeDtypeStruct((8 * CELLS, 128), F32),
            jax.ShapeDtypeStruct((D, D), F32),
        ],
        in_specs=[ANY] * 3,
        out_specs=[ANY] * 3,
        scratch_shapes=[DMA((PLANE - 1,))] * 4 + [DMA((PIECES,))] * 5 + [DMA((3,))],
        compiler_params=remote(1),
        name="scatter",
    )(buffer, counts, start_basis[0])
    partial = pl.pallas_call(
        moments_kernel,
        out_shape=jax.ShapeDtypeStruct((PACKED, RB), F32),
        in_specs=[VMEM, VMEM],
        out_specs=VMEM,
        compiler_params=params(40),
        name="moments",
    )(received, got_counts)
    reduced = pl.pallas_call(
        reduce_kernel,
        out_shape=jax.ShapeDtypeStruct((PACKED, RB), F32),
        in_specs=[VMEM],
        out_specs=VMEM,
        scratch_shapes=[
            pltpu.VMEM((PACKED, RB), F32),
            pltpu.VMEM((HALF, RB), F32),
            pltpu.VMEM((HALF, RB), F32),
            pltpu.VMEM((RING, CHUNK, RB), F32),
            DMA, DMA,
        ] + [DMA((RING,))] * 6,
        compiler_params=remote(2),
        name="reduce",
    )(partial)
    rotation, shift = sweeps(reduced, basis)
    rotated = pl.pallas_call(
        rotate_kernel,
        out_shape=jax.ShapeDtypeStruct((SLOTS, D), BF16),
        in_specs=[VMEM] * 3,
        out_specs=VMEM,
        compiler_params=params(40),
        name="rotate",
    )(received, rotation, shift)
    returned = pl.pallas_call(
        giveback_kernel,
        out_shape=jax.ShapeDtypeStruct((SLOTS, D), BF16),
        in_specs=[ANY],
        out_specs=ANY,
        scratch_shapes=[DMA((PLANE - 1,))] * 2 + [DMA((1,))],
        compiler_params=remote(3),
        name="giveback",
    )(rotated)
    return pl.pallas_call(
        collect_kernel,
        out_shape=jax.ShapeDtypeStruct((ROWS, D), BF16),
        in_specs=[VMEM] * 2,
        out_specs=VMEM,
        compiler_params=params(40),
        name="collect",
    )(returned, place)


def solution(mesh):
    both = P(("bucket", "replica"), None)
    return jax.shard_map(
        body,
        mesh=mesh,
        in_specs=(both, both, P("bucket", None, None)),
        out_specs=both,
        check_vma=False,
    )
```

```python
import functools

import jax
import jax.numpy as jnp
from jax import lax
from jax.experimental import pallas as pl
from jax.experimental.pallas import tpu as pltpu
from jax.sharding import PartitionSpec as P

CELLS = 16
SWEEPS = 3
CAP = 128
D = 768
RB = 128
NB = D // RB
ROWS = 1024
SLOTS = CELLS * CAP
F32 = jnp.float32
BF16 = jnp.bfloat16
NT = (((1,), (1,)), ((), ()))
TN = (((0,), (0,)), ((), ()))
VMEM = pl.BlockSpec(memory_space=pltpu.VMEM)
ANY = pl.BlockSpec(memory_space=pl.ANY)
MESH = pl.DeviceIdType.MESH
DMA = pltpu.SemaphoreType.DMA
PLANE = 16
RING = 8
PAIRS = [(i, j) for i in range(NB) for j in range(i, NB)]
CHUNK = 176
HALF = RING * CHUNK
PACKED = 2 * HALF
TAIL = len(PAIRS) * RB
PIECES = 12
PIECE = D // PIECES


def params(mib, **kw):
    return pltpu.CompilerParams(vmem_limit_bytes=mib * 2**20, **kw)


def dot(a, b):
    return jnp.dot(a, b, preferred_element_type=F32)


def dot_nt(a, b):
    return lax.dot_general(a, b, NT, preferred_element_type=F32)


def side(parts):
    return jnp.concatenate(parts, axis=1)


def pile(parts):
    return jnp.concatenate(parts, axis=0)


def thirds(x):
    high = x.astype(BF16)
    left = x - high.astype(F32)
    middle = left.astype(BF16)
    return high, middle, (left - middle.astype(F32)).astype(BF16)


def halves(x):
    high = x.astype(BF16)
    return high, (x - high.astype(F32)).astype(BF16)


def dispatch_kernel(ids_ref, rows_ref, buffer_ref, counts_ref, place_ref):
    ids = ids_ref[...]
    cells = lax.broadcasted_iota(jnp.int32, (CELLS, ROWS), 0)
    onehot = (ids == cells).astype(F32)
    before = (
        lax.broadcasted_iota(jnp.int32, (ROWS, ROWS), 0)
        < lax.broadcasted_iota(jnp.int32, (ROWS, ROWS), 1)
    ).astype(F32).astype(BF16)
    ranks = dot(onehot.astype(BF16), before)
    slot = jnp.sum(ranks * onehot, axis=0, keepdims=True).astype(jnp.int32)
    place = ids * CAP + slot
    eighth = lax.broadcasted_iota(jnp.int32, (8 * CELLS, ROWS), 0) // 8
    each = jnp.sum((ids == eighth).astype(F32), axis=1, keepdims=True)
    counts_ref[...] = jnp.broadcast_to(each, (8 * CELLS, 128))
    place_ref[...] = jnp.broadcast_to(place, (128, ROWS)).T

    def fill(cell, carry):
        wanted = lax.broadcasted_iota(jnp.int32, (CAP, ROWS), 0) + cell * CAP
        pick = (place == wanted).astype(F32).astype(BF16)
        first = pl.multiple_of(cell * CAP, CAP)
        buffer_ref[pl.ds(first, CAP), :] = dot(pick, rows_ref[...]).astype(BF16)
        return carry

    lax.fori_loop(0, CELLS, fill, 0)


def scatter_kernel(
    buffer_ref, counts_ref, basis_ref, received_ref, got_counts_ref, got_basis_ref,
    send, recv, send_count, recv_count, send_up, send_down, send_across, recv_chain, recv_across, own
):
    bucket, me = lax.axis_index("bucket"), lax.axis_index("replica")
    z, core = bucket // 2, bucket % 2
    origin, chain_core = me // 2, me % 2
    away = lax.rem(z + RING - origin, RING)
    up = lax.rem(z + 1, RING) * 2 + core
    down = lax.rem(z + RING - 1, RING) * 2 + core
    across = z * 2 + (1 - core)
    peers = plane_peers(me)

    barrier = pltpu.get_barrier_semaphore()
    for peer in peers:
        pl.semaphore_signal(barrier, inc=1, device_id=(bucket, peer), device_id_type=MESH)
    for other in (up, down, across):
        pl.semaphore_signal(barrier, inc=1, device_id=(other, me), device_id_type=MESH)
    pl.semaphore_wait(barrier, len(peers) + 3)

    copies = []
    for index, peer in enumerate(peers):
        copies.append(pltpu.make_async_remote_copy(
            counts_ref.at[pl.ds(pl.multiple_of(peer * 8, 8), 8)],
            got_counts_ref.at[pl.ds(pl.multiple_of(me * 8, 8), 8)],
            send_count.at[index], recv_count.at[index], device_id=(bucket, peer), device_id_type=MESH,
        ))
        copies.append(exchange(buffer_ref, received_ref, send, recv, index, bucket, me, peer))
    for copy in copies:
        copy.start()
    mine = pl.ds(pl.multiple_of(me * CAP, CAP), CAP)
    mine_counts = pl.ds(pl.multiple_of(me * 8, 8), 8)
    local = [
        pltpu.make_async_copy(buffer_ref.at[mine], received_ref.at[mine], own.at[0]),
        pltpu.make_async_copy(counts_ref.at[mine_counts], got_counts_ref.at[mine_counts], own.at[1]),
    ]
    for copy in local:
        copy.start()

    def passing(source, index, sends, receives, target):
        span = pl.ds(index * PIECE, PIECE)
        return pltpu.make_async_remote_copy(
            source.at[span], got_basis_ref.at[span], sends.at[index], receives.at[index],
            device_id=(target, me), device_id_type=MESH,
        )

    on_chain = core == chain_core
    first = on_chain & (away == 0)
    later = on_chain & (away > 0)

    @pl.when(first)
    def _():
        whole = pltpu.make_async_copy(basis_ref, got_basis_ref, own.at[2])
        whole.start()
        for index in range(PIECES):
            passing(basis_ref, index, send_up, recv_chain, up).start()
            passing(basis_ref, index, send_down, recv_chain, down).start()
            passing(basis_ref, index, send_across, recv_across, across).start()
        for index in range(PIECES):
            passing(basis_ref, index, send_up, recv_chain, up).wait_send()
            passing(basis_ref, index, send_down, recv_chain, down).wait_send()
            passing(basis_ref, index, send_across, recv_across, across).wait_send()
        whole.wait()

    @pl.when(later)
    def _():
        upward = away < 4
        downward = away > 5
        for index in range(PIECES):
            passing(got_basis_ref, index, send_up, recv_chain, up).wait_recv()

            @pl.when(upward)
            def _():
                passing(got_basis_ref, index, send_up, recv_chain, up).start()

            @pl.when(downward)
            def _():
                passing(got_basis_ref, index, send_down, recv_chain, down).start()

            passing(got_basis_ref, index, send_across, recv_across, across).start()
        for index in range(PIECES):
            @pl.when(upward)
            def _():
                passing(got_basis_ref, index, send_up, recv_chain, up).wait_send()

            @pl.when(downward)
            def _():
                passing(got_basis_ref, index, send_down, recv_chain, down).wait_send()

            passing(got_basis_ref, index, send_across, recv_across, across).wait_send()

    @pl.when(core != chain_core)
    def _():
        for index in range(PIECES):
            passing(got_basis_ref, index, send_across, recv_across, across).wait_recv()

    for copy in copies + local:
        copy.wait()


def plane_peers(me):
    y, x = me // 4, me % 4
    return [
        lax.rem(y + dy, 4) * 4 + lax.rem(x + dx, 4)
        for dy, dx in sorted(
            ((dy, dx) for dy in range(4) for dx in range(4) if dy or dx),
            key=lambda o: -min(o[0], 4 - o[0]) - min(o[1], 4 - o[1]),
        )
    ]


def exchange(source, target, send, recv, index, bucket, me, peer):
    return pltpu.make_async_remote_copy(
        source.at[pl.ds(pl.multiple_of(peer * CAP, CAP), CAP)],
        target.at[pl.ds(pl.multiple_of(me * CAP, CAP), CAP)],
        send.at[index], recv.at[index], device_id=(bucket, peer), device_id_type=MESH,
    )


def giveback_kernel(rotated_ref, returned_ref, send, recv, own):
    bucket, me = lax.axis_index("bucket"), lax.axis_index("replica")
    peers = plane_peers(me)
    barrier = pltpu.get_barrier_semaphore()
    for peer in peers:
        pl.semaphore_signal(barrier, inc=1, device_id=(bucket, peer), device_id_type=MESH)
    pl.semaphore_wait(barrier, len(peers))
    copies = [
        exchange(rotated_ref, returned_ref, send, recv, index, bucket, me, peer)
        for index, peer in enumerate(peers)
    ]
    mine = pl.ds(pl.multiple_of(me * CAP, CAP), CAP)
    copies.append(pltpu.make_async_copy(rotated_ref.at[mine], returned_ref.at[mine], own.at[0]))
    for copy in copies:
        copy.start()
    for copy in copies:
        copy.wait()


def moments_kernel(received_ref, counts_ref, out_ref):
    place = 0
    for block in range(NB):
        rest = slice(block * RB, D)
        square = lax.dot_general(
            received_ref[:, block * RB : block * RB + RB], received_ref[:, rest], TN,
            preferred_element_type=F32,
        )
        for other in range(NB - block):
            out_ref[place : place + RB, :] = square[:, other * RB : other * RB + RB]
            place += RB
    total = dot(jnp.ones((8, SLOTS), BF16), received_ref[...])
    out_ref[TAIL:PACKED, :] = jnp.zeros((PACKED - TAIL, RB), F32)
    for block in range(NB):
        out_ref[TAIL + block : TAIL + block + 1, :] = total[0:1, block * RB : block * RB + RB]
    count = jnp.sum(counts_ref[...].reshape(CELLS, 8, 128)[:, 0, :], axis=0, keepdims=True)
    out_ref[TAIL + NB : TAIL + NB + 1, :] = count


def reduce_kernel(
    part_ref, out_ref, full, arrived, mine, slots, send_half, recv_half, send_part, recv_part,
    send_all, recv_all, send_across, recv_across
):
    bucket, me = lax.axis_index("bucket"), lax.axis_index("replica")
    z, core = bucket // 2, bucket % 2
    across = (z * 2 + (1 - core), me)
    ring = [(lax.rem(z + step, RING) * 2 + core, me) for step in range(RING)]
    barrier = pltpu.get_barrier_semaphore()
    for other in [across] + ring[1:]:
        pl.semaphore_signal(barrier, inc=1, device_id=other, device_id_type=MESH)
    pl.semaphore_wait(barrier, RING)

    half = pltpu.make_async_remote_copy(
        part_ref.at[pl.ds(pl.multiple_of((1 - core) * HALF, 8), HALF)], arrived,
        send_half, recv_half, device_id=across, device_id_type=MESH,
    )
    half.start()
    half.wait()
    mine[...] = part_ref[pl.ds(pl.multiple_of(core * HALF, 8), HALF), :] + arrived[...]

    order = [4, 3, 5, 2, 6, 1, 7]
    parts = []
    for step in order:
        chunk = lax.rem(z + step, RING)
        parts.append(pltpu.make_async_remote_copy(
            mine.at[pl.ds(pl.multiple_of(chunk * CHUNK, 8), CHUNK)], slots.at[step],
            send_part.at[step], recv_part.at[step], device_id=ring[step], device_id_type=MESH,
        ))
    for copy in parts:
        copy.start()
    total = mine[pl.ds(pl.multiple_of(z * CHUNK, 8), CHUNK), :]
    for step, copy in zip(order, parts):
        copy.wait_recv()
        total = total + slots[step]

    def chunk_of(where):
        return pl.ds(pl.multiple_of((core * RING + where) * CHUNK, 8), CHUNK)

    full[chunk_of(z), :] = total
    spread = [
        pltpu.make_async_remote_copy(
            full.at[chunk_of(z)], full.at[chunk_of(z)], send_all.at[step], recv_all.at[step],
            device_id=ring[step], device_id_type=MESH,
        )
        for step in order
    ]
    for copy in spread:
        copy.start()

    def forward(step):
        where = chunk_of(lax.rem(z + RING - step, RING))
        return pltpu.make_async_remote_copy(
            full.at[where], full.at[where], send_across.at[step], recv_across.at[step],
            device_id=across, device_id_type=MESH,
        )

    forward(0).start()
    for step, copy in sorted(zip(order, spread), key=lambda item: min(item[0], RING - item[0])):
        copy.wait_recv()
        forward(step).start()
    for step in range(RING):
        forward(step).wait()
    for copy in parts + spread:
        copy.wait_send()
    out_ref[...] = full[...]


def factor(a_ref, m_ref):
    n = RB // 8
    shape = (8, RB)
    sub = lax.broadcasted_iota(jnp.int32, shape, 0)
    lane = lax.broadcasted_iota(jnp.int32, shape, 1)
    x = [a_ref[8 * r : 8 * r + 8, :] for r in range(n)]

    def wide(v):
        return jnp.broadcast_to(v, shape)

    def assemble(v):
        out = v[0]
        for j in range(1, 8):
            out = jnp.where(sub == j, v[j], out)
        return out

    for b in range(n):
        near = min(b + 2, n)
        inside = (lane >= 8 * b) & (lane < 8 * b + 8)
        col = {
            r: [wide(x[r][:, 8 * b + j : 8 * b + j + 1]) for j in range(8)] for r in range(b, near)
        }
        s = [
            [wide(col[b][j][i : i + 1, :]) if i >= j else None for j in range(8)] for i in range(8)
        ]
        t = [[None] * 8 for _ in range(8)]
        inverse = [None] * 8
        for j in range(0, 8, 2):
            p, q, w = s[j][j], s[j + 1][j], s[j + 1][j + 1]
            inverse[j] = 1.0 / p
            t[j + 1][j] = q * inverse[j]
            both = 1.0 / (p * w - q * q)
            inverse[j + 1] = p * both
            for i in range(j + 2, 8):
                t[i][j] = s[i][j] * inverse[j]
                t[i][j + 1] = (s[i][j + 1] * p - s[i][j] * q) * both
            for k in range(j + 2, 8):
                g0 = (s[k][j] * w - s[k][j + 1] * q) * both
                for i in range(k, 8):
                    s[i][k] = s[i][k] - g0 * s[i][j] - t[k][j + 1] * s[i][j + 1]
            s[j + 1][j + 1] = w - t[j + 1][j] * q
        low = {}
        for r in range(b, near):
            c = list(col[r])
            low[r] = []
            for j in range(8):
                for i in range(j + 1, 8):
                    c[i] = c[i] - c[j] * t[i][j]
                low[r].append(c[j] * inverse[j])
        panel = jnp.where(inside, (lane == sub + 8 * b).astype(F32), x[b])
        rows = []
        for j in range(8):
            rows.append(wide(panel[j : j + 1, :]))
            if j < 7:
                panel = panel - jnp.where(sub > j, low[b][j], 0.0) * rows[j]
        pivots = assemble([s[j][j] for j in range(8)])
        x[b] = jnp.where(lane < 8 * b + 8, panel * lax.rsqrt(pivots), 0.0)
        for r in range(b + 1, near):
            even, odd = low[r][0] * rows[0], low[r][1] * rows[1]
            for j in range(2, 8, 2):
                even = even + low[r][j] * rows[j]
                odd = odd + low[r][j + 1] * rows[j + 1]
            x[r] = jnp.where(inside, 0.0, x[r]) - (even + odd)
        if near < n:
            g = [rows[j] * inverse[j] for j in range(8)]
            for j in range(7, 0, -1):
                for i in range(j):
                    g[i] = g[i] - t[j][i] * g[j]
            above = [jnp.zeros((8 * b, RB), F32)] if b else []
            below = [jnp.zeros((RB - 8 * b - 8, RB), F32)]
            g_high, g_low = halves(jnp.concatenate(above + [assemble(g)] + below, axis=0))
            x_high, x_low = halves(jnp.concatenate(x[near:], axis=0))
            change = dot(x_high, g_high) + dot(x_high, g_low) + dot(x_low, g_high)
            for r in range(near, n):
                first = 8 * (r - near)
                x[r] = jnp.where(inside, 0.0, x[r]) - change[first : first + 8, :]
    for r in range(n):
        m_ref[8 * r : 8 * r + 8, :] = x[r]


def sweeps_kernel(
    reduced_ref, start_ref, w_high, shift_ref, c_high, c_low, y, y_high, y_low, w_low, gram, inverse
):
    count = reduced_ref[TAIL + NB : TAIL + NB + 1, :]
    divisor = jnp.maximum(count, 1.0)
    mean = jnp.concatenate(
        [reduced_ref[TAIL + block : TAIL + block + 1, :] / divisor for block in range(NB)], axis=1
    )
    m1, m2, m3 = thirds(jnp.broadcast_to(mean, (16, D)))
    row = lax.broadcasted_iota(jnp.int32, (16, D), 0)
    nothing = jnp.zeros((16, D), F32)
    m1, m2, m3 = m1.astype(F32), m2.astype(F32), m3.astype(F32)

    def stack(parts):
        out = nothing
        for index, part in enumerate(parts):
            out = jnp.where(row == index, part, out)
        return out.astype(BF16)

    mean_left = stack([m1, m1, m2, m1, m3, m2])
    mean_right = stack([m1, m2, m1, m3, m1, m2])
    for block in range(NB):
        span = slice(block * RB, block * RB + RB)
        outer = lax.dot_general(
            mean_left[:, span], mean_right, TN, preferred_element_type=F32,
        )
        for other in range(NB):
            columns = slice(other * RB, other * RB + RB)
            place = PAIRS.index((min(block, other), max(block, other))) * RB
            piece = reduced_ref[place : place + RB, :]
            if other < block:
                piece = piece.T
            high, low = halves(piece / divisor - outer[:, columns])
            c_high[span, columns] = high
            c_low[span, columns] = low
        high, low = halves(start_ref[:, span].T)
        w_high[span, :] = high
        w_low[span, :] = low

    def sweep(step, carry):
        for block in range(D // 256):
            span = slice(block * 256, block * 256 + 256)
            high, low = w_high[span, :], w_low[span, :]
            image = dot(side([high, high, low]), pile([c_high[...], c_low[...], c_high[...]]))
            y[span, :] = image
            high, low = halves(image)
            y_high[span, :] = high
            y_low[span, :] = low

        last = step == SWEEPS - 1

        def block_step(block, inner):
            span = pl.ds(pl.multiple_of(block * RB, RB), RB)

            @pl.when(jnp.logical_not(last))
            def _():
                gram[...] = dot_nt(y_high[span, :], y_high[span, :])

            @pl.when(last)
            def _():
                high, low = y_high[span, :], y_low[span, :]
                gram[...] = dot_nt(side([high, high, low]), side([high, low, high]))

            factor(gram, inverse)
            i_high, i_low = halves(inverse[...])

            def keep(own):
                high, low = halves(own)
                w_high[span, :] = high
                w_low[span, :] = low

            @pl.when(jnp.logical_not(last))
            def _():
                keep(dot(side([i_high, i_high]), pile([y_high[span, :], y_low[span, :]])))

            @pl.when(last)
            def _():
                high, low = y_high[span, :], y_low[span, :]
                keep(dot(side([i_high, i_high, i_low]), pile([high, low, high])))

            for done in range(NB - 1):
                rest = slice(RB * (done + 1), D)
                own = slice(RB * done, RB * done + RB)

                def remove(change, rest=rest):
                    left = y[rest, :] - change
                    y[rest, :] = left
                    high, low = halves(left)
                    y_high[rest, :] = high
                    y_low[rest, :] = low

                @pl.when((block == done) & jnp.logical_not(last))
                def _(rest=rest, own=own, remove=remove):
                    u_h, u_l = w_high[own, :], w_low[own, :]
                    l_h = dot_nt(y_high[rest, :], u_h).astype(BF16)
                    remove(dot(side([l_h, l_h]), pile([u_h, u_l])))

                @pl.when((block == done) & last)
                def _(rest=rest, own=own, remove=remove):
                    u_h, u_l = w_high[own, :], w_low[own, :]
                    r_h, r_l = y_high[rest, :], y_low[rest, :]
                    l_h, l_l = halves(dot_nt(side([r_h, r_h, r_l]), side([u_h, u_l, u_h])))
                    remove(dot(side([l_h, l_h, l_l]), pile([u_h, u_l, u_h])))

            return inner

        return lax.fori_loop(0, NB, block_step, carry)

    lax.fori_loop(0, SWEEPS, sweep, 0)
    shifts = dot_nt(stack([m1, m2, m3]), w_high[...])
    shift_ref[...] = jnp.broadcast_to(shifts[0:1, :] + shifts[1:2, :] + shifts[2:3, :], (8, D))


def rotate_kernel(received_ref, w_ref, shift_ref, out_ref):
    def step(index, carry):
        span = pl.ds(pl.multiple_of(index * 256, 256), 256)
        product = dot_nt(received_ref[span, :], w_ref[...])
        out_ref[span, :] = (product - shift_ref[0:1, :]).astype(BF16)
        return carry

    lax.fori_loop(0, SLOTS // 256, step, 0)


def collect_kernel(returned_ref, place_ref, out_ref):
    def step(index, carry):
        span = pl.ds(pl.multiple_of(index * 256, 256), 256)
        place = place_ref[span, :]
        lane = lax.broadcasted_iota(jnp.int32, (256, CAP), 1)
        pick = jnp.concatenate(
            [(place == lane + cell * CAP).astype(F32).astype(BF16) for cell in range(CELLS)], axis=1
        )
        out_ref[span, :] = dot(pick, returned_ref[...]).astype(BF16)
        return carry

    lax.fori_loop(0, ROWS // 256, step, 0)


def sweeps(reduced, start):
    return pl.pallas_call(
        sweeps_kernel,
        out_shape=[jax.ShapeDtypeStruct((D, D), BF16), jax.ShapeDtypeStruct((8, D), F32)],
        in_specs=[VMEM, VMEM],
        out_specs=[VMEM, VMEM],
        scratch_shapes=[
            pltpu.VMEM((D, D), BF16),
            pltpu.VMEM((D, D), BF16),
            pltpu.VMEM((D, D), F32),
            pltpu.VMEM((D, D), BF16),
            pltpu.VMEM((D, D), BF16),
            pltpu.VMEM((D, D), BF16),
            pltpu.VMEM((RB, RB), F32),
            pltpu.VMEM((RB, RB), F32),
        ],
        compiler_params=params(48),
        name="sweeps",
    )(reduced, start)


def remote(identity):
    return params(40, collective_id=identity, has_side_effects=True)


def body(rows, cell_ids, start_basis):
    buffer, counts, place = pl.pallas_call(
        dispatch_kernel,
        out_shape=[
            jax.ShapeDtypeStruct((SLOTS, D), BF16),
            jax.ShapeDtypeStruct((8 * CELLS, 128), F32),
            jax.ShapeDtypeStruct((ROWS, 128), jnp.int32),
        ],
        in_specs=[VMEM, VMEM],
        out_specs=[VMEM] * 3,
        compiler_params=params(40),
        name="dispatch",
    )(cell_ids.reshape(1, ROWS), rows)
    received, got_counts, basis = pl.pallas_call(
        scatter_kernel,
        out_shape=[
            jax.ShapeDtypeStruct((SLOTS, D), BF16),
            jax.ShapeDtypeStruct((8 * CELLS, 128), F32),
            jax.ShapeDtypeStruct((D, D), F32),
        ],
        in_specs=[ANY] * 3,
        out_specs=[ANY] * 3,
        scratch_shapes=[DMA((PLANE - 1,))] * 4 + [DMA((PIECES,))] * 5 + [DMA((3,))],
        compiler_params=remote(1),
        name="scatter",
    )(buffer, counts, start_basis[0])
    partial = pl.pallas_call(
        moments_kernel,
        out_shape=jax.ShapeDtypeStruct((PACKED, RB), F32),
        in_specs=[VMEM, VMEM],
        out_specs=VMEM,
        compiler_params=params(40),
        name="moments",
    )(received, got_counts)
    reduced = pl.pallas_call(
        reduce_kernel,
        out_shape=jax.ShapeDtypeStruct((PACKED, RB), F32),
        in_specs=[VMEM],
        out_specs=VMEM,
        scratch_shapes=[
            pltpu.VMEM((PACKED, RB), F32),
            pltpu.VMEM((HALF, RB), F32),
            pltpu.VMEM((HALF, RB), F32),
            pltpu.VMEM((RING, CHUNK, RB), F32),
            DMA, DMA,
        ] + [DMA((RING,))] * 6,
        compiler_params=remote(2),
        name="reduce",
    )(partial)
    rotation, shift = sweeps(reduced, basis)
    rotated = pl.pallas_call(
        rotate_kernel,
        out_shape=jax.ShapeDtypeStruct((SLOTS, D), BF16),
        in_specs=[VMEM] * 3,
        out_specs=VMEM,
        compiler_params=params(40),
        name="rotate",
    )(received, rotation, shift)
    returned = pl.pallas_call(
        giveback_kernel,
        out_shape=jax.ShapeDtypeStruct((SLOTS, D), BF16),
        in_specs=[ANY],
        out_specs=ANY,
        scratch_shapes=[DMA((PLANE - 1,))] * 2 + [DMA((1,))],
        compiler_params=remote(3),
        name="giveback",
    )(rotated)
    return pl.pallas_call(
        collect_kernel,
        out_shape=jax.ShapeDtypeStruct((ROWS, D), BF16),
        in_specs=[VMEM] * 2,
        out_specs=VMEM,
        compiler_params=params(40),
        name="collect",
    )(returned, place)


def solution(mesh):
    both = P(("bucket", "replica"), None)
    return jax.shard_map(
        body,
        mesh=mesh,
        in_specs=(both, both, P("bucket", None, None)),
        out_specs=both,
        check_vma=False,
    )
```

```python
import functools

import jax
import jax.numpy as jnp
from jax import lax
from jax.experimental import pallas as pl
from jax.experimental.pallas import tpu as pltpu
from jax.sharding import PartitionSpec as P

CELLS = 16
SWEEPS = 3
CAP = 128
D = 768
RB = 128
NB = D // RB
ROWS = 1024
SLOTS = CELLS * CAP
F32 = jnp.float32
BF16 = jnp.bfloat16
NT = (((1,), (1,)), ((), ()))
TN = (((0,), (0,)), ((), ()))
VMEM = pl.BlockSpec(memory_space=pltpu.VMEM)
ANY = pl.BlockSpec(memory_space=pl.ANY)
MESH = pl.DeviceIdType.MESH
DMA = pltpu.SemaphoreType.DMA
PLANE = 16
RING = 8
PAIRS = [(i, j) for i in range(NB) for j in range(i, NB)]
CHUNK = 176
HALF = RING * CHUNK
PACKED = 2 * HALF
TAIL = len(PAIRS) * RB
PIECES = 12
ORDER = (
    (0, 1), (2, 2), (1, 0), (1, 2), (0, 3), (2, 1), (3, 0), (2, 3),
    (1, 1), (0, 2), (3, 3), (2, 0), (1, 3), (3, 2), (3, 1),
)
PIECE = D // PIECES


def params(mib, **kw):
    return pltpu.CompilerParams(vmem_limit_bytes=mib * 2**20, **kw)


def dot(a, b):
    return jnp.dot(a, b, preferred_element_type=F32)


def dot_nt(a, b):
    return lax.dot_general(a, b, NT, preferred_element_type=F32)


def side(parts):
    return jnp.concatenate(parts, axis=1)


def pile(parts):
    return jnp.concatenate(parts, axis=0)


def thirds(x):
    high = x.astype(BF16)
    left = x - high.astype(F32)
    middle = left.astype(BF16)
    return high, middle, (left - middle.astype(F32)).astype(BF16)


def halves(x):
    high = x.astype(BF16)
    return high, (x - high.astype(F32)).astype(BF16)


def scatter_kernel(
    ids_ref, rows_ref, basis_ref, received_ref, got_counts_ref, got_basis_ref, place_ref,
    buffer, counts,
    send, recv, send_count, recv_count, send_up, send_down, send_across, recv_chain, recv_across, own
):
    bucket, me = lax.axis_index("bucket"), lax.axis_index("replica")
    z, core = bucket // 2, bucket % 2
    origin, chain_core = me // 2, me % 2
    away = lax.rem(z + RING - origin, RING)
    up = lax.rem(z + 1, RING) * 2 + core
    down = lax.rem(z + RING - 1, RING) * 2 + core
    across = z * 2 + (1 - core)
    peers = plane_peers(me)

    barrier = pltpu.get_barrier_semaphore()
    for peer in peers:
        pl.semaphore_signal(barrier, inc=1, device_id=(bucket, peer), device_id_type=MESH)
    for other in (up, down, across):
        pl.semaphore_signal(barrier, inc=1, device_id=(other, me), device_id_type=MESH)
    pl.semaphore_wait(barrier, len(peers) + 3)

    def passing(source, index, sends, receives, target):
        span = pl.ds(index * PIECE, PIECE)
        return pltpu.make_async_remote_copy(
            source.at[span], got_basis_ref.at[span], sends.at[index], receives.at[index],
            device_id=(target, me), device_id_type=MESH,
        )

    on_chain = core == chain_core
    first = on_chain & (away == 0)
    later = on_chain & (away > 0)

    whole = pltpu.make_async_copy(basis_ref, got_basis_ref, own.at[2])

    @pl.when(first)
    def _():
        for index in range(PIECES):
            passing(basis_ref, index, send_up, recv_chain, up).start()
            passing(basis_ref, index, send_down, recv_chain, down).start()
            passing(basis_ref, index, send_across, recv_across, across).start()
        whole.start()

    ids = ids_ref[...]
    cells = lax.broadcasted_iota(jnp.int32, (CELLS, ROWS), 0)
    onehot = (ids == cells).astype(F32)
    before = (
        lax.broadcasted_iota(jnp.int32, (ROWS, ROWS), 0)
        < lax.broadcasted_iota(jnp.int32, (ROWS, ROWS), 1)
    ).astype(F32).astype(BF16)
    ranks = dot(onehot.astype(BF16), before)
    slot = jnp.sum(ranks * onehot, axis=0, keepdims=True).astype(jnp.int32)
    place = ids * CAP + slot
    eighth = lax.broadcasted_iota(jnp.int32, (8 * CELLS, ROWS), 0) // 8
    each = jnp.sum((ids == eighth).astype(F32), axis=1, keepdims=True)
    counts[...] = jnp.broadcast_to(each, (8 * CELLS, 128))

    def fill(cell):
        wanted = lax.broadcasted_iota(jnp.int32, (CAP, ROWS), 0) + cell * CAP
        pick = (place == wanted).astype(F32).astype(BF16)
        start = pl.multiple_of(cell * CAP, CAP)
        buffer[pl.ds(start, CAP), :] = dot(pick, rows_ref[...]).astype(BF16)

    copies = []
    for index, peer in enumerate(peers):
        fill(peer)
        copies.append(exchange(buffer, received_ref, send, recv, index, bucket, me, peer))
        copies[-1].start()
    fill(me)
    for index, peer in enumerate(peers):
        copies.append(pltpu.make_async_remote_copy(
            counts.at[pl.ds(pl.multiple_of(peer * 8, 8), 8)],
            got_counts_ref.at[pl.ds(pl.multiple_of(me * 8, 8), 8)],
            send_count.at[index], recv_count.at[index], device_id=(bucket, peer), device_id_type=MESH,
        ))
        copies[-1].start()
    mine = pl.ds(pl.multiple_of(me * CAP, CAP), CAP)
    mine_counts = pl.ds(pl.multiple_of(me * 8, 8), 8)
    local = [
        pltpu.make_async_copy(buffer.at[mine], received_ref.at[mine], own.at[0]),
        pltpu.make_async_copy(counts.at[mine_counts], got_counts_ref.at[mine_counts], own.at[1]),
    ]
    for copy in local:
        copy.start()
    place_ref[...] = jnp.broadcast_to(place, (128, ROWS)).T

    @pl.when(first)
    def _():
        for index in range(PIECES):
            passing(basis_ref, index, send_up, recv_chain, up).wait_send()
            passing(basis_ref, index, send_down, recv_chain, down).wait_send()
            passing(basis_ref, index, send_across, recv_across, across).wait_send()
        whole.wait()

    @pl.when(later)
    def _():
        upward = away < 4
        downward = away > 5
        for index in range(PIECES):
            passing(got_basis_ref, index, send_up, recv_chain, up).wait_recv()

            @pl.when(upward)
            def _():
                passing(got_basis_ref, index, send_up, recv_chain, up).start()

            @pl.when(downward)
            def _():
                passing(got_basis_ref, index, send_down, recv_chain, down).start()

            passing(got_basis_ref, index, send_across, recv_across, across).start()
        for index in range(PIECES):
            @pl.when(upward)
            def _():
                passing(got_basis_ref, index, send_up, recv_chain, up).wait_send()

            @pl.when(downward)
            def _():
                passing(got_basis_ref, index, send_down, recv_chain, down).wait_send()

            passing(got_basis_ref, index, send_across, recv_across, across).wait_send()

    @pl.when(core != chain_core)
    def _():
        for index in range(PIECES):
            passing(got_basis_ref, index, send_across, recv_across, across).wait_recv()

    for copy in copies + local:
        copy.wait()


def plane_peers(me):
    y, x = me // 4, me % 4
    return [
        lax.rem(y + dy, 4) * 4 + lax.rem(x + dx, 4)
        for dy, dx in ORDER
    ]


def exchange(source, target, send, recv, index, bucket, me, peer):
    return pltpu.make_async_remote_copy(
        source.at[pl.ds(pl.multiple_of(peer * CAP, CAP), CAP)],
        target.at[pl.ds(pl.multiple_of(me * CAP, CAP), CAP)],
        send.at[index], recv.at[index], device_id=(bucket, peer), device_id_type=MESH,
    )


def giveback_kernel(received_ref, w_ref, shift_ref, returned_ref, rotated, send, recv, own):
    bucket, me = lax.axis_index("bucket"), lax.axis_index("replica")
    peers = plane_peers(me)
    barrier = pltpu.get_barrier_semaphore()
    for peer in peers:
        pl.semaphore_signal(barrier, inc=1, device_id=(bucket, peer), device_id_type=MESH)
    pl.semaphore_wait(barrier, len(peers))

    def block(peer):
        return pl.ds(pl.multiple_of(peer * CAP, CAP), CAP)

    copies = []
    order = peers + [me]
    for index in range(0, PLANE, 2):
        pair = order[index : index + 2]
        product = dot_nt(pile([received_ref[block(peer), :] for peer in pair]), w_ref[...])
        values = (product - shift_ref[0:1, :]).astype(BF16)
        for half, peer in enumerate(pair):
            rotated[block(peer), :] = values[half * CAP : half * CAP + CAP, :]
            if index + half < PLANE - 1:
                copies.append(
                    exchange(rotated, returned_ref, send, recv, index + half, bucket, me, peer)
                )
            else:
                copies.append(
                    pltpu.make_async_copy(rotated.at[block(me)], returned_ref.at[block(me)], own.at[0])
                )
            copies[-1].start()
    for copy in copies:
        copy.wait()


def moments_kernel(received_ref, counts_ref, out_ref):
    place = 0
    for block in range(NB):
        rest = slice(block * RB, D)
        square = lax.dot_general(
            received_ref[:, block * RB : block * RB + RB], received_ref[:, rest], TN,
            preferred_element_type=F32,
        )
        for other in range(NB - block):
            out_ref[place : place + RB, :] = square[:, other * RB : other * RB + RB]
            place += RB
    total = dot(jnp.ones((8, SLOTS), BF16), received_ref[...])
    out_ref[TAIL:PACKED, :] = jnp.zeros((PACKED - TAIL, RB), F32)
    for block in range(NB):
        out_ref[TAIL + block : TAIL + block + 1, :] = total[0:1, block * RB : block * RB + RB]
    count = jnp.sum(counts_ref[...].reshape(CELLS, 8, 128)[:, 0, :], axis=0, keepdims=True)
    out_ref[TAIL + NB : TAIL + NB + 1, :] = count


def reduce_kernel(
    part_ref, out_ref, full, arrived, mine, slots, send_half, recv_half, send_part, recv_part,
    send_all, recv_all, send_across, recv_across
):
    bucket, me = lax.axis_index("bucket"), lax.axis_index("replica")
    z, core = bucket // 2, bucket % 2
    across = (z * 2 + (1 - core), me)
    ring = [(lax.rem(z + step, RING) * 2 + core, me) for step in range(RING)]
    barrier = pltpu.get_barrier_semaphore()
    for other in [across] + ring[1:]:
        pl.semaphore_signal(barrier, inc=1, device_id=other, device_id_type=MESH)
    pl.semaphore_wait(barrier, RING)

    def rows_of(chunk):
        return pl.ds(pl.multiple_of(chunk * CHUNK, 8), CHUNK)

    order = [1, 7, 2, 6, 3, 5, 4]
    halves_out = {}
    for step in order + [0]:
        chunk = lax.rem(z + step, RING)
        halves_out[step] = pltpu.make_async_remote_copy(
            part_ref.at[rows_of((1 - core) * RING + chunk)], arrived.at[rows_of(chunk)],
            send_half.at[step], recv_half.at[step], device_id=across, device_id_type=MESH,
        )
        halves_out[step].start()

    def add_pair(step):
        chunk = lax.rem(z + step, RING)
        halves_out[step].wait_recv()
        mine[rows_of(chunk), :] = part_ref[rows_of(core * RING + chunk), :] + arrived[rows_of(chunk), :]

    parts = []
    for step in order:
        add_pair(step)
        parts.append(pltpu.make_async_remote_copy(
            mine.at[rows_of(lax.rem(z + step, RING))], slots.at[step],
            send_part.at[step], recv_part.at[step], device_id=ring[step], device_id_type=MESH,
        ))
        parts[-1].start()
    add_pair(0)
    total = mine[rows_of(z), :]
    for step, copy in zip(order, parts):
        copy.wait_recv()
        total = total + slots[step]

    def chunk_of(where):
        return pl.ds(pl.multiple_of((core * RING + where) * CHUNK, 8), CHUNK)

    full[chunk_of(z), :] = total
    spread = [
        pltpu.make_async_remote_copy(
            full.at[chunk_of(z)], full.at[chunk_of(z)], send_all.at[step], recv_all.at[step],
            device_id=ring[step], device_id_type=MESH,
        )
        for step in order
    ]
    for copy in spread:
        copy.start()

    def forward(step):
        where = chunk_of(lax.rem(z + RING - step, RING))
        return pltpu.make_async_remote_copy(
            full.at[where], full.at[where], send_across.at[step], recv_across.at[step],
            device_id=across, device_id_type=MESH,
        )

    forward(0).start()
    for step, copy in sorted(zip(order, spread), key=lambda item: min(item[0], RING - item[0])):
        copy.wait_recv()
        forward(step).start()
    for step in range(RING):
        forward(step).wait()
    for copy in parts + spread + list(halves_out.values()):
        copy.wait_send()
    out_ref[...] = full[...]


def factor(a_ref, m_ref):
    n = RB // 8
    shape = (8, RB)
    sub = lax.broadcasted_iota(jnp.int32, shape, 0)
    lane = lax.broadcasted_iota(jnp.int32, shape, 1)
    x = [a_ref[8 * r : 8 * r + 8, :] for r in range(n)]

    def wide(v):
        return jnp.broadcast_to(v, shape)

    def assemble(v):
        out = v[0]
        for j in range(1, 8):
            out = jnp.where(sub == j, v[j], out)
        return out

    for b in range(n):
        near = min(b + 2, n)
        inside = (lane >= 8 * b) & (lane < 8 * b + 8)
        col = {
            r: [wide(x[r][:, 8 * b + j : 8 * b + j + 1]) for j in range(8)] for r in range(b, near)
        }
        s = [
            [wide(col[b][j][i : i + 1, :]) if i >= j else None for j in range(8)] for i in range(8)
        ]
        t = [[None] * 8 for _ in range(8)]
        inverse = [None] * 8
        for j in range(0, 8, 2):
            p, q, w = s[j][j], s[j + 1][j], s[j + 1][j + 1]
            inverse[j] = 1.0 / p
            t[j + 1][j] = q * inverse[j]
            both = 1.0 / (p * w - q * q)
            inverse[j + 1] = p * both
            for i in range(j + 2, 8):
                t[i][j] = s[i][j] * inverse[j]
                t[i][j + 1] = (s[i][j + 1] * p - s[i][j] * q) * both
            for k in range(j + 2, 8):
                g0 = (s[k][j] * w - s[k][j + 1] * q) * both
                for i in range(k, 8):
                    s[i][k] = s[i][k] - g0 * s[i][j] - t[k][j + 1] * s[i][j + 1]
            s[j + 1][j + 1] = w - t[j + 1][j] * q
        low = {}
        for r in range(b, near):
            c = list(col[r])
            low[r] = []
            for j in range(8):
                for i in range(j + 1, 8):
                    c[i] = c[i] - c[j] * t[i][j]
                low[r].append(c[j] * inverse[j])
        panel = jnp.where(inside, (lane == sub + 8 * b).astype(F32), x[b])
        rows = []
        for j in range(8):
            rows.append(wide(panel[j : j + 1, :]))
            if j < 7:
                panel = panel - jnp.where(sub > j, low[b][j], 0.0) * rows[j]
        pivots = assemble([s[j][j] for j in range(8)])
        x[b] = jnp.where(lane < 8 * b + 8, panel * lax.rsqrt(pivots), 0.0)
        for r in range(b + 1, near):
            even, odd = low[r][0] * rows[0], low[r][1] * rows[1]
            for j in range(2, 8, 2):
                even = even + low[r][j] * rows[j]
                odd = odd + low[r][j + 1] * rows[j + 1]
            x[r] = jnp.where(inside, 0.0, x[r]) - (even + odd)
        if near < n:
            g = [rows[j] * inverse[j] for j in range(8)]
            for j in range(7, 0, -1):
                for i in range(j):
                    g[i] = g[i] - t[j][i] * g[j]
            above = [jnp.zeros((8 * b, RB), F32)] if b else []
            below = [jnp.zeros((RB - 8 * b - 8, RB), F32)]
            g_high, g_low = halves(jnp.concatenate(above + [assemble(g)] + below, axis=0))
            x_high, x_low = halves(jnp.concatenate(x[near:], axis=0))
            change = dot(x_high, g_high) + dot(x_high, g_low) + dot(x_low, g_high)
            for r in range(near, n):
                first = 8 * (r - near)
                x[r] = jnp.where(inside, 0.0, x[r]) - change[first : first + 8, :]
    for r in range(n):
        m_ref[8 * r : 8 * r + 8, :] = x[r]


def sweeps_kernel(
    reduced_ref, start_ref, w_high, shift_ref, c_high, c_low, y, y_high, y_low, w_low, gram, inverse
):
    count = reduced_ref[TAIL + NB : TAIL + NB + 1, :]
    divisor = jnp.maximum(count, 1.0)
    mean = jnp.concatenate(
        [reduced_ref[TAIL + block : TAIL + block + 1, :] / divisor for block in range(NB)], axis=1
    )
    m1, m2, m3 = thirds(jnp.broadcast_to(mean, (16, D)))
    row = lax.broadcasted_iota(jnp.int32, (16, D), 0)
    nothing = jnp.zeros((16, D), F32)
    m1, m2, m3 = m1.astype(F32), m2.astype(F32), m3.astype(F32)

    def stack(parts):
        out = nothing
        for index, part in enumerate(parts):
            out = jnp.where(row == index, part, out)
        return out.astype(BF16)

    mean_left = stack([m1, m1, m2, m1, m3, m2])
    mean_right = stack([m1, m2, m1, m3, m1, m2])
    for block in range(NB):
        span = slice(block * RB, block * RB + RB)
        outer = lax.dot_general(
            mean_left[:, span], mean_right, TN, preferred_element_type=F32,
        )
        for other in range(NB):
            columns = slice(other * RB, other * RB + RB)
            place = PAIRS.index((min(block, other), max(block, other))) * RB
            piece = reduced_ref[place : place + RB, :]
            if other < block:
                piece = piece.T
            high, low = halves(piece / divisor - outer[:, columns])
            c_high[span, columns] = high
            c_low[span, columns] = low
        high, low = halves(start_ref[:, span].T)
        w_high[span, :] = high
        w_low[span, :] = low

    def sweep(step, carry):
        for block in range(D // 256):
            span = slice(block * 256, block * 256 + 256)
            high, low = w_high[span, :], w_low[span, :]
            image = dot(side([high, high, low]), pile([c_high[...], c_low[...], c_high[...]]))
            y[span, :] = image
            high, low = halves(image)
            y_high[span, :] = high
            y_low[span, :] = low

        last = step == SWEEPS - 1

        def block_step(block, inner):
            span = pl.ds(pl.multiple_of(block * RB, RB), RB)

            @pl.when(jnp.logical_not(last))
            def _():
                gram[...] = dot_nt(y_high[span, :], y_high[span, :])

            @pl.when(last)
            def _():
                high, low = y_high[span, :], y_low[span, :]
                gram[...] = dot_nt(side([high, high, low]), side([high, low, high]))

            factor(gram, inverse)
            i_high, i_low = halves(inverse[...])

            def keep(own):
                high, low = halves(own)
                w_high[span, :] = high
                w_low[span, :] = low

            @pl.when(jnp.logical_not(last))
            def _():
                keep(dot(side([i_high, i_high]), pile([y_high[span, :], y_low[span, :]])))

            @pl.when(last)
            def _():
                high, low = y_high[span, :], y_low[span, :]
                keep(dot(side([i_high, i_high, i_low]), pile([high, low, high])))

            for done in range(NB - 1):
                rest = slice(RB * (done + 1), D)
                own = slice(RB * done, RB * done + RB)

                def remove(change, rest=rest):
                    left = y[rest, :] - change
                    y[rest, :] = left
                    high, low = halves(left)
                    y_high[rest, :] = high
                    y_low[rest, :] = low

                @pl.when((block == done) & jnp.logical_not(last))
                def _(rest=rest, own=own, remove=remove):
                    u_h, u_l = w_high[own, :], w_low[own, :]
                    l_h = dot_nt(y_high[rest, :], u_h).astype(BF16)
                    remove(dot(side([l_h, l_h]), pile([u_h, u_l])))

                @pl.when((block == done) & last)
                def _(rest=rest, own=own, remove=remove):
                    u_h, u_l = w_high[own, :], w_low[own, :]
                    r_h, r_l = y_high[rest, :], y_low[rest, :]
                    l_h, l_l = halves(dot_nt(side([r_h, r_h, r_l]), side([u_h, u_l, u_h])))
                    remove(dot(side([l_h, l_h, l_l]), pile([u_h, u_l, u_h])))

            return inner

        return lax.fori_loop(0, NB, block_step, carry)

    lax.fori_loop(0, SWEEPS, sweep, 0)
    shifts = dot_nt(stack([m1, m2, m3]), w_high[...])
    shift_ref[...] = jnp.broadcast_to(shifts[0:1, :] + shifts[1:2, :] + shifts[2:3, :], (8, D))


def collect_kernel(returned_ref, place_ref, out_ref):
    def step(index, carry):
        span = pl.ds(pl.multiple_of(index * 256, 256), 256)
        place = place_ref[span, :]
        lane = lax.broadcasted_iota(jnp.int32, (256, CAP), 1)
        pick = jnp.concatenate(
            [(place == lane + cell * CAP).astype(F32).astype(BF16) for cell in range(CELLS)], axis=1
        )
        out_ref[span, :] = dot(pick, returned_ref[...]).astype(BF16)
        return carry

    lax.fori_loop(0, ROWS // 256, step, 0)


def sweeps(reduced, start):
    return pl.pallas_call(
        sweeps_kernel,
        out_shape=[jax.ShapeDtypeStruct((D, D), BF16), jax.ShapeDtypeStruct((8, D), F32)],
        in_specs=[VMEM, VMEM],
        out_specs=[VMEM, VMEM],
        scratch_shapes=[
            pltpu.VMEM((D, D), BF16),
            pltpu.VMEM((D, D), BF16),
            pltpu.VMEM((D, D), F32),
            pltpu.VMEM((D, D), BF16),
            pltpu.VMEM((D, D), BF16),
            pltpu.VMEM((D, D), BF16),
            pltpu.VMEM((RB, RB), F32),
            pltpu.VMEM((RB, RB), F32),
        ],
        compiler_params=params(48),
        name="sweeps",
    )(reduced, start)


def remote(identity):
    return params(40, collective_id=identity, has_side_effects=True)


def body(rows, cell_ids, start_basis):
    received, got_counts, basis, place = pl.pallas_call(
        scatter_kernel,
        out_shape=[
            jax.ShapeDtypeStruct((SLOTS, D), BF16),
            jax.ShapeDtypeStruct((8 * CELLS, 128), F32),
            jax.ShapeDtypeStruct((D, D), F32),
            jax.ShapeDtypeStruct((ROWS, 128), jnp.int32),
        ],
        in_specs=[VMEM, VMEM, ANY],
        out_specs=[ANY] * 3 + [VMEM],
        scratch_shapes=[pltpu.VMEM((SLOTS, D), BF16), pltpu.VMEM((8 * CELLS, 128), F32)]
        + [DMA((PLANE - 1,))] * 4 + [DMA((PIECES,))] * 5 + [DMA((3,))],
        compiler_params=remote(1),
        name="scatter",
    )(cell_ids.reshape(1, ROWS), rows, start_basis[0])
    partial = pl.pallas_call(
        moments_kernel,
        out_shape=jax.ShapeDtypeStruct((PACKED, RB), F32),
        in_specs=[VMEM, VMEM],
        out_specs=VMEM,
        compiler_params=params(40),
        name="moments",
    )(received, got_counts)
    reduced = pl.pallas_call(
        reduce_kernel,
        out_shape=jax.ShapeDtypeStruct((PACKED, RB), F32),
        in_specs=[VMEM],
        out_specs=VMEM,
        scratch_shapes=[
            pltpu.VMEM((PACKED, RB), F32),
            pltpu.VMEM((HALF, RB), F32),
            pltpu.VMEM((HALF, RB), F32),
            pltpu.VMEM((RING, CHUNK, RB), F32),
        ] + [DMA((RING,))] * 8,
        compiler_params=remote(2),
        name="reduce",
    )(partial)
    rotation, shift = sweeps(reduced, basis)
    returned = pl.pallas_call(
        giveback_kernel,
        out_shape=jax.ShapeDtypeStruct((SLOTS, D), BF16),
        in_specs=[VMEM] * 3,
        out_specs=ANY,
        scratch_shapes=[pltpu.VMEM((SLOTS, D), BF16)] + [DMA((PLANE - 1,))] * 2 + [DMA((1,))],
        compiler_params=remote(3),
        name="giveback",
    )(received, rotation, shift)
    return pl.pallas_call(
        collect_kernel,
        out_shape=jax.ShapeDtypeStruct((ROWS, D), BF16),
        in_specs=[VMEM] * 2,
        out_specs=VMEM,
        compiler_params=params(40),
        name="collect",
    )(returned, place)


def solution(mesh):
    both = P(("bucket", "replica"), None)
    return jax.shard_map(
        body,
        mesh=mesh,
        in_specs=(both, both, P("bucket", None, None)),
        out_specs=both,
        check_vma=False,
    )
```

```python
import functools

import jax
import jax.numpy as jnp
from jax import lax
from jax.experimental import pallas as pl
from jax.experimental.pallas import tpu as pltpu
from jax.sharding import PartitionSpec as P

CELLS = 16
SWEEPS = 3
CAP = 128
D = 768
RB = 128
NB = D // RB
ROWS = 1024
SLOTS = CELLS * CAP
F32 = jnp.float32
BF16 = jnp.bfloat16
NT = (((1,), (1,)), ((), ()))
TN = (((0,), (0,)), ((), ()))
VMEM = pl.BlockSpec(memory_space=pltpu.VMEM)
ANY = pl.BlockSpec(memory_space=pl.ANY)
MESH = pl.DeviceIdType.MESH
DMA = pltpu.SemaphoreType.DMA
PLANE = 16
RING = 8
PAIRS = [(i, j) for i in range(NB) for j in range(i, NB)]
CHUNK = 176
HALF = RING * CHUNK
PACKED = 2 * HALF
TAIL = len(PAIRS) * RB
PIECES = 12
ORDER = (
    (0, 1), (2, 2), (1, 0), (1, 2), (0, 3), (2, 1), (3, 0), (2, 3),
    (1, 1), (0, 2), (3, 3), (2, 0), (1, 3), (3, 2), (3, 1),
)
PIECE = D // PIECES


def params(mib, **kw):
    return pltpu.CompilerParams(vmem_limit_bytes=mib * 2**20, **kw)


def dot(a, b):
    return jnp.dot(a, b, preferred_element_type=F32)


def dot_nt(a, b):
    return lax.dot_general(a, b, NT, preferred_element_type=F32)


def side(parts):
    return jnp.concatenate(parts, axis=1)


def pile(parts):
    return jnp.concatenate(parts, axis=0)


def thirds(x):
    high = x.astype(BF16)
    left = x - high.astype(F32)
    middle = left.astype(BF16)
    return high, middle, (left - middle.astype(F32)).astype(BF16)


def halves(x):
    high = x.astype(BF16)
    return high, (x - high.astype(F32)).astype(BF16)


def scatter_kernel(
    ids_ref, rows_ref, basis_ref, received_ref, got_counts_ref, got_basis_ref, place_ref,
    buffer, counts,
    send, recv, send_count, recv_count, send_up, send_down, send_across, recv_chain, recv_across, own
):
    bucket, me = lax.axis_index("bucket"), lax.axis_index("replica")
    z, core = bucket // 2, bucket % 2
    origin, chain_core = me // 2, me % 2
    away = lax.rem(z + RING - origin, RING)
    up = lax.rem(z + 1, RING) * 2 + core
    down = lax.rem(z + RING - 1, RING) * 2 + core
    across = z * 2 + (1 - core)
    peers = plane_peers(me)

    barrier = pltpu.get_barrier_semaphore()
    for peer in peers:
        pl.semaphore_signal(barrier, inc=1, device_id=(bucket, peer), device_id_type=MESH)
    for other in (up, down, across):
        pl.semaphore_signal(barrier, inc=1, device_id=(other, me), device_id_type=MESH)
    pl.semaphore_wait(barrier, len(peers) + 3)

    def passing(source, index, sends, receives, target):
        span = pl.ds(index * PIECE, PIECE)
        return pltpu.make_async_remote_copy(
            source.at[span], got_basis_ref.at[span], sends.at[index], receives.at[index],
            device_id=(target, me), device_id_type=MESH,
        )

    on_chain = core == chain_core
    first = on_chain & (away == 0)
    later = on_chain & (away > 0)

    whole = pltpu.make_async_copy(basis_ref, got_basis_ref, own.at[2])

    @pl.when(first)
    def _():
        for index in range(PIECES):
            passing(basis_ref, index, send_up, recv_chain, up).start()
            passing(basis_ref, index, send_down, recv_chain, down).start()
            passing(basis_ref, index, send_across, recv_across, across).start()
        whole.start()

    ids = ids_ref[...]
    cells = lax.broadcasted_iota(jnp.int32, (CELLS, ROWS), 0)
    onehot = (ids == cells).astype(F32)
    before = (
        lax.broadcasted_iota(jnp.int32, (ROWS, ROWS), 0)
        < lax.broadcasted_iota(jnp.int32, (ROWS, ROWS), 1)
    ).astype(F32).astype(BF16)
    ranks = dot(onehot.astype(BF16), before)
    slot = jnp.sum(ranks * onehot, axis=0, keepdims=True).astype(jnp.int32)
    place = ids * CAP + slot
    eighth = lax.broadcasted_iota(jnp.int32, (8 * CELLS, ROWS), 0) // 8
    each = jnp.sum((ids == eighth).astype(F32), axis=1, keepdims=True)
    counts[...] = jnp.broadcast_to(each, (8 * CELLS, 128))

    def fill(cell):
        wanted = lax.broadcasted_iota(jnp.int32, (CAP, ROWS), 0) + cell * CAP
        pick = (place == wanted).astype(F32).astype(BF16)
        start = pl.multiple_of(cell * CAP, CAP)
        buffer[pl.ds(start, CAP), :] = dot(pick, rows_ref[...]).astype(BF16)

    copies = []
    for index, peer in enumerate(peers):
        fill(peer)
        copies.append(exchange(buffer, received_ref, send, recv, index, bucket, me, peer))
        copies[-1].start()
    fill(me)
    for index, peer in enumerate(peers):
        copies.append(pltpu.make_async_remote_copy(
            counts.at[pl.ds(pl.multiple_of(peer * 8, 8), 8)],
            got_counts_ref.at[pl.ds(pl.multiple_of(me * 8, 8), 8)],
            send_count.at[index], recv_count.at[index], device_id=(bucket, peer), device_id_type=MESH,
        ))
        copies[-1].start()
    mine = pl.ds(pl.multiple_of(me * CAP, CAP), CAP)
    mine_counts = pl.ds(pl.multiple_of(me * 8, 8), 8)
    local = [
        pltpu.make_async_copy(buffer.at[mine], received_ref.at[mine], own.at[0]),
        pltpu.make_async_copy(counts.at[mine_counts], got_counts_ref.at[mine_counts], own.at[1]),
    ]
    for copy in local:
        copy.start()
    place_ref[...] = jnp.broadcast_to(place, (128, ROWS)).T

    @pl.when(first)
    def _():
        for index in range(PIECES):
            passing(basis_ref, index, send_up, recv_chain, up).wait_send()
            passing(basis_ref, index, send_down, recv_chain, down).wait_send()
            passing(basis_ref, index, send_across, recv_across, across).wait_send()
        whole.wait()

    @pl.when(later)
    def _():
        upward = away < 4
        downward = away > 5
        for index in range(PIECES):
            passing(got_basis_ref, index, send_up, recv_chain, up).wait_recv()

            @pl.when(upward)
            def _():
                passing(got_basis_ref, index, send_up, recv_chain, up).start()

            @pl.when(downward)
            def _():
                passing(got_basis_ref, index, send_down, recv_chain, down).start()

            passing(got_basis_ref, index, send_across, recv_across, across).start()
        for index in range(PIECES):
            @pl.when(upward)
            def _():
                passing(got_basis_ref, index, send_up, recv_chain, up).wait_send()

            @pl.when(downward)
            def _():
                passing(got_basis_ref, index, send_down, recv_chain, down).wait_send()

            passing(got_basis_ref, index, send_across, recv_across, across).wait_send()

    @pl.when(core != chain_core)
    def _():
        for index in range(PIECES):
            passing(got_basis_ref, index, send_across, recv_across, across).wait_recv()

    for copy in copies + local:
        copy.wait()


def plane_peers(me):
    y, x = me // 4, me % 4
    return [
        lax.rem(y + dy, 4) * 4 + lax.rem(x + dx, 4)
        for dy, dx in ORDER
    ]


def exchange(source, target, send, recv, index, bucket, me, peer):
    return pltpu.make_async_remote_copy(
        source.at[pl.ds(pl.multiple_of(peer * CAP, CAP), CAP)],
        target.at[pl.ds(pl.multiple_of(me * CAP, CAP), CAP)],
        send.at[index], recv.at[index], device_id=(bucket, peer), device_id_type=MESH,
    )


def giveback_kernel(received_ref, w_ref, shift_ref, returned_ref, rotated, send, recv, own):
    bucket, me = lax.axis_index("bucket"), lax.axis_index("replica")
    peers = plane_peers(me)
    barrier = pltpu.get_barrier_semaphore()
    for peer in peers:
        pl.semaphore_signal(barrier, inc=1, device_id=(bucket, peer), device_id_type=MESH)
    pl.semaphore_wait(barrier, len(peers))

    def block(peer):
        return pl.ds(pl.multiple_of(peer * CAP, CAP), CAP)

    copies = []
    order = peers + [me]
    for index in range(0, PLANE, 2):
        pair = order[index : index + 2]
        product = dot_nt(pile([received_ref[block(peer), :] for peer in pair]), w_ref[...])
        values = (product - shift_ref[0:1, :]).astype(BF16)
        for half, peer in enumerate(pair):
            rotated[block(peer), :] = values[half * CAP : half * CAP + CAP, :]
            if index + half < PLANE - 1:
                copies.append(
                    exchange(rotated, returned_ref, send, recv, index + half, bucket, me, peer)
                )
            else:
                copies.append(
                    pltpu.make_async_copy(rotated.at[block(me)], returned_ref.at[block(me)], own.at[0])
                )
            copies[-1].start()
    for copy in copies:
        copy.wait()


def moments_kernel(received_ref, counts_ref, out_ref):
    place = 0
    for block in range(NB):
        rest = slice(block * RB, D)
        square = lax.dot_general(
            received_ref[:, block * RB : block * RB + RB], received_ref[:, rest], TN,
            preferred_element_type=F32,
        )
        for other in range(NB - block):
            out_ref[place : place + RB, :] = square[:, other * RB : other * RB + RB]
            place += RB
    total = dot(jnp.ones((8, SLOTS), BF16), received_ref[...])
    out_ref[TAIL:PACKED, :] = jnp.zeros((PACKED - TAIL, RB), F32)
    for block in range(NB):
        out_ref[TAIL + block : TAIL + block + 1, :] = total[0:1, block * RB : block * RB + RB]
    count = jnp.sum(counts_ref[...].reshape(CELLS, 8, 128)[:, 0, :], axis=0, keepdims=True)
    out_ref[TAIL + NB : TAIL + NB + 1, :] = count


def reduce_kernel(
    part_ref, out_ref, full, arrived, mine, slots, send_half, recv_half, send_part, recv_part,
    send_all, recv_all, send_across, recv_across
):
    bucket, me = lax.axis_index("bucket"), lax.axis_index("replica")
    z, core = bucket // 2, bucket % 2
    across = (z * 2 + (1 - core), me)
    ring = [(lax.rem(z + step, RING) * 2 + core, me) for step in range(RING)]
    barrier = pltpu.get_barrier_semaphore()
    for other in [across] + ring[1:]:
        pl.semaphore_signal(barrier, inc=1, device_id=other, device_id_type=MESH)
    pl.semaphore_wait(barrier, RING)

    def rows_of(chunk):
        return pl.ds(pl.multiple_of(chunk * CHUNK, 8), CHUNK)

    order = [1, 7, 2, 6, 3, 5, 4]
    halves_out = {}
    for step in order + [0]:
        chunk = lax.rem(z + step, RING)
        halves_out[step] = pltpu.make_async_remote_copy(
            part_ref.at[rows_of((1 - core) * RING + chunk)], arrived.at[rows_of(chunk)],
            send_half.at[step], recv_half.at[step], device_id=across, device_id_type=MESH,
        )
        halves_out[step].start()

    def add_pair(step):
        chunk = lax.rem(z + step, RING)
        halves_out[step].wait_recv()
        mine[rows_of(chunk), :] = part_ref[rows_of(core * RING + chunk), :] + arrived[rows_of(chunk), :]

    parts = []
    for step in order:
        add_pair(step)
        parts.append(pltpu.make_async_remote_copy(
            mine.at[rows_of(lax.rem(z + step, RING))], slots.at[step],
            send_part.at[step], recv_part.at[step], device_id=ring[step], device_id_type=MESH,
        ))
        parts[-1].start()
    add_pair(0)
    total = mine[rows_of(z), :]
    for step, copy in zip(order, parts):
        copy.wait_recv()
        total = total + slots[step]

    def chunk_of(where):
        return pl.ds(pl.multiple_of((core * RING + where) * CHUNK, 8), CHUNK)

    full[chunk_of(z), :] = total
    spread = [
        pltpu.make_async_remote_copy(
            full.at[chunk_of(z)], full.at[chunk_of(z)], send_all.at[step], recv_all.at[step],
            device_id=ring[step], device_id_type=MESH,
        )
        for step in order
    ]
    for copy in spread:
        copy.start()

    def forward(step):
        where = chunk_of(lax.rem(z + RING - step, RING))
        return pltpu.make_async_remote_copy(
            full.at[where], full.at[where], send_across.at[step], recv_across.at[step],
            device_id=across, device_id_type=MESH,
        )

    forward(0).start()
    for step, copy in sorted(zip(order, spread), key=lambda item: min(item[0], RING - item[0])):
        copy.wait_recv()
        forward(step).start()
    for step in range(RING):
        forward(step).wait()
    for copy in parts + spread + list(halves_out.values()):
        copy.wait_send()
    out_ref[...] = full[...]


def factor(a_ref, m_ref, columns):
    n = RB // 8
    shape = (8, RB)
    sub = lax.broadcasted_iota(jnp.int32, shape, 0)
    lane = lax.broadcasted_iota(jnp.int32, shape, 1)
    x = [a_ref[8 * r : 8 * r + 8, :] for r in range(n)]

    def wide(v):
        return jnp.broadcast_to(v, shape)

    def assemble(v):
        out = v[0]
        for j in range(1, 8):
            out = jnp.where(sub == j, v[j], out)
        return out

    for b in range(n):
        near = min(b + 2, n)
        inside = (lane >= 8 * b) & (lane < 8 * b + 8)
        col = {
            r: [wide(x[r][:, 8 * b + j : 8 * b + j + 1]) for j in range(8)] for r in range(b, near)
        }
        base = 64 * (b % 2)
        for j in range(8):
            columns[base + 8 * j : base + 8 * j + 8, :] = col[b][j]
        s = [
            [columns[pl.ds(base + 8 * j + i, 8, stride=0), :] if i >= j else None for j in range(8)]
            for i in range(8)
        ]
        t = [[None] * 8 for _ in range(8)]
        inverse = [None] * 8
        for j in range(0, 8, 2):
            p, q, w = s[j][j], s[j + 1][j], s[j + 1][j + 1]
            inverse[j] = 1.0 / p
            t[j + 1][j] = q * inverse[j]
            both = 1.0 / (p * w - q * q)
            inverse[j + 1] = p * both
            for i in range(j + 2, 8):
                t[i][j] = s[i][j] * inverse[j]
                t[i][j + 1] = (s[i][j + 1] * p - s[i][j] * q) * both
            for k in range(j + 2, 8):
                g0 = (s[k][j] * w - s[k][j + 1] * q) * both
                for i in range(k, 8):
                    s[i][k] = s[i][k] - g0 * s[i][j] - t[k][j + 1] * s[i][j + 1]
            s[j + 1][j + 1] = w - t[j + 1][j] * q
        low = {}
        for r in range(b, near):
            c = list(col[r])
            low[r] = []
            for j in range(8):
                for i in range(j + 1, 8):
                    c[i] = c[i] - c[j] * t[i][j]
                low[r].append(c[j] * inverse[j])
        panel = jnp.where(inside, (lane == sub + 8 * b).astype(F32), x[b])
        rows = []
        for j in range(8):
            rows.append(wide(panel[j : j + 1, :]))
            if j < 7:
                panel = panel - jnp.where(sub > j, low[b][j], 0.0) * rows[j]
        pivots = assemble([s[j][j] for j in range(8)])
        x[b] = jnp.where(lane < 8 * b + 8, panel * lax.rsqrt(pivots), 0.0)
        for r in range(b + 1, near):
            even, odd = low[r][0] * rows[0], low[r][1] * rows[1]
            for j in range(2, 8, 2):
                even = even + low[r][j] * rows[j]
                odd = odd + low[r][j + 1] * rows[j + 1]
            x[r] = jnp.where(inside, 0.0, x[r]) - (even + odd)
        if near < n:
            g = [rows[j] * inverse[j] for j in range(8)]
            for j in range(7, 0, -1):
                for i in range(j):
                    g[i] = g[i] - t[j][i] * g[j]
            above = [jnp.zeros((8 * b, RB), F32)] if b else []
            below = [jnp.zeros((RB - 8 * b - 8, RB), F32)]
            g_high, g_low = halves(jnp.concatenate(above + [assemble(g)] + below, axis=0))
            x_high, x_low = halves(jnp.concatenate(x[near:], axis=0))
            two = dot(x_high, side([g_high, g_low]))
            change = two[:, :RB] + two[:, RB:] + dot(x_low, g_high)
            for r in range(near, n):
                first = 8 * (r - near)
                x[r] = jnp.where(inside, 0.0, x[r]) - change[first : first + 8, :]
    for r in range(n):
        m_ref[8 * r : 8 * r + 8, :] = x[r]


def sweeps_kernel(
    reduced_ref, start_ref, w_high, shift_ref, c_high, c_low, y, y_high, y_low, w_low, gram, inverse, spread_columns
):
    count = reduced_ref[TAIL + NB : TAIL + NB + 1, :]
    divisor = jnp.maximum(count, 1.0)
    mean = jnp.concatenate(
        [reduced_ref[TAIL + block : TAIL + block + 1, :] / divisor for block in range(NB)], axis=1
    )
    m1, m2, m3 = thirds(jnp.broadcast_to(mean, (16, D)))
    row = lax.broadcasted_iota(jnp.int32, (16, D), 0)
    nothing = jnp.zeros((16, D), F32)
    m1, m2, m3 = m1.astype(F32), m2.astype(F32), m3.astype(F32)

    def stack(parts):
        out = nothing
        for index, part in enumerate(parts):
            out = jnp.where(row == index, part, out)
        return out.astype(BF16)

    mean_left = stack([m1, m1, m2, m1, m3, m2])
    mean_right = stack([m1, m2, m1, m3, m1, m2])
    for block in range(NB):
        span = slice(block * RB, block * RB + RB)
        outer = lax.dot_general(
            mean_left[:, span], mean_right, TN, preferred_element_type=F32,
        )
        for other in range(NB):
            columns = slice(other * RB, other * RB + RB)
            place = PAIRS.index((min(block, other), max(block, other))) * RB
            piece = reduced_ref[place : place + RB, :]
            if other < block:
                piece = piece.T
            high, low = halves(piece / divisor - outer[:, columns])
            c_high[span, columns] = high
            c_low[span, columns] = low
        high, low = halves(start_ref[:, span].T)
        w_high[span, :] = high
        w_low[span, :] = low

    def sweep(step, carry):
        for block in range(D // 256):
            span = slice(block * 256, block * 256 + 256)
            high, low = w_high[span, :], w_low[span, :]
            image = dot(side([high, high, low]), pile([c_high[...], c_low[...], c_high[...]]))
            y[span, :] = image
            high, low = halves(image)
            y_high[span, :] = high
            y_low[span, :] = low
            if block == 0:
                high, low = high[:RB, :], low[:RB, :]
                gram[...] = dot_nt(side([high, high, low]), side([high, low, high]))

        last = step == SWEEPS - 1

        def block_step(block, inner):
            factor(gram, inverse, spread_columns)

            def finish(done, exact):
                own = slice(RB * done, RB * done + RB)
                high, low = y_high[own, :], y_low[own, :]
                i_high, i_low = halves(inverse[...])
                if exact:
                    kept = dot(side([i_high, i_high, i_low]), pile([high, low, high]))
                else:
                    kept = dot(side([i_high, i_high]), pile([high, low]))
                u_h, u_l = halves(kept)
                w_high[own, :] = u_h
                w_low[own, :] = u_l
                if done == NB - 1:
                    return
                rest = slice(RB * (done + 1), D)
                if exact:
                    r_h, r_l = y_high[rest, :], y_low[rest, :]
                    l_h, l_l = halves(dot_nt(side([r_h, r_h, r_l]), side([u_h, u_l, u_h])))
                    change = dot(side([l_h, l_h, l_l]), pile([u_h, u_l, u_h]))
                else:
                    l_h = dot_nt(y_high[rest, :], u_h).astype(BF16)
                    change = dot(side([l_h, l_h]), pile([u_h, u_l]))
                left = y[rest, :] - change
                high, low = halves(left)
                y[rest, :] = left
                y_high[rest, :] = high
                y_low[rest, :] = low
                high, low = high[:RB, :], low[:RB, :]
                if exact:
                    gram[...] = dot_nt(side([high, high, low]), side([high, low, high]))
                else:
                    gram[...] = dot_nt(high, high)

            for done in range(NB):
                pl.when((block == done) & jnp.logical_not(last))(
                    functools.partial(finish, done, False)
                )
                pl.when((block == done) & last)(functools.partial(finish, done, True))
            return inner

        return lax.fori_loop(0, NB, block_step, carry)

    lax.fori_loop(0, SWEEPS, sweep, 0)
    shifts = dot_nt(stack([m1, m2, m3]), w_high[...])
    shift_ref[...] = jnp.broadcast_to(shifts[0:1, :] + shifts[1:2, :] + shifts[2:3, :], (8, D))


def collect_kernel(returned_ref, place_ref, out_ref):
    def step(index, carry):
        span = pl.ds(pl.multiple_of(index * 256, 256), 256)
        place = place_ref[span, :]
        lane = lax.broadcasted_iota(jnp.int32, (256, CAP), 1)
        pick = jnp.concatenate(
            [(place == lane + cell * CAP).astype(F32).astype(BF16) for cell in range(CELLS)], axis=1
        )
        out_ref[span, :] = dot(pick, returned_ref[...]).astype(BF16)
        return carry

    lax.fori_loop(0, ROWS // 256, step, 0)


def sweeps(reduced, start):
    return pl.pallas_call(
        sweeps_kernel,
        out_shape=[jax.ShapeDtypeStruct((D, D), BF16), jax.ShapeDtypeStruct((8, D), F32)],
        in_specs=[VMEM, VMEM],
        out_specs=[VMEM, VMEM],
        scratch_shapes=[
            pltpu.VMEM((D, D), BF16),
            pltpu.VMEM((D, D), BF16),
            pltpu.VMEM((D, D), F32),
            pltpu.VMEM((D, D), BF16),
            pltpu.VMEM((D, D), BF16),
            pltpu.VMEM((D, D), BF16),
            pltpu.VMEM((RB, RB), F32),
            pltpu.VMEM((RB, RB), F32),
            pltpu.VMEM((RB + 8, RB), F32),
        ],
        compiler_params=params(48),
        name="sweeps",
    )(reduced, start)


def remote(identity):
    return params(40, collective_id=identity, has_side_effects=True)


def body(rows, cell_ids, start_basis):
    received, got_counts, basis, place = pl.pallas_call(
        scatter_kernel,
        out_shape=[
            jax.ShapeDtypeStruct((SLOTS, D), BF16),
            jax.ShapeDtypeStruct((8 * CELLS, 128), F32),
            jax.ShapeDtypeStruct((D, D), F32),
            jax.ShapeDtypeStruct((ROWS, 128), jnp.int32),
        ],
        in_specs=[VMEM, VMEM, ANY],
        out_specs=[ANY] * 3 + [VMEM],
        scratch_shapes=[pltpu.VMEM((SLOTS, D), BF16), pltpu.VMEM((8 * CELLS, 128), F32)]
        + [DMA((PLANE - 1,))] * 4 + [DMA((PIECES,))] * 5 + [DMA((3,))],
        compiler_params=remote(1),
        name="scatter",
    )(cell_ids.reshape(1, ROWS), rows, start_basis[0])
    partial = pl.pallas_call(
        moments_kernel,
        out_shape=jax.ShapeDtypeStruct((PACKED, RB), F32),
        in_specs=[VMEM, VMEM],
        out_specs=VMEM,
        compiler_params=params(40),
        name="moments",
    )(received, got_counts)
    reduced = pl.pallas_call(
        reduce_kernel,
        out_shape=jax.ShapeDtypeStruct((PACKED, RB), F32),
        in_specs=[VMEM],
        out_specs=VMEM,
        scratch_shapes=[
            pltpu.VMEM((PACKED, RB), F32),
            pltpu.VMEM((HALF, RB), F32),
            pltpu.VMEM((HALF, RB), F32),
            pltpu.VMEM((RING, CHUNK, RB), F32),
        ] + [DMA((RING,))] * 8,
        compiler_params=remote(2),
        name="reduce",
    )(partial)
    rotation, shift = sweeps(reduced, basis)
    returned = pl.pallas_call(
        giveback_kernel,
        out_shape=jax.ShapeDtypeStruct((SLOTS, D), BF16),
        in_specs=[VMEM] * 3,
        out_specs=ANY,
        scratch_shapes=[pltpu.VMEM((SLOTS, D), BF16)] + [DMA((PLANE - 1,))] * 2 + [DMA((1,))],
        compiler_params=remote(3),
        name="giveback",
    )(received, rotation, shift)
    return pl.pallas_call(
        collect_kernel,
        out_shape=jax.ShapeDtypeStruct((ROWS, D), BF16),
        in_specs=[VMEM] * 2,
        out_specs=VMEM,
        compiler_params=params(40),
        name="collect",
    )(returned, place)


def solution(mesh):
    both = P(("bucket", "replica"), None)
    return jax.shard_map(
        body,
        mesh=mesh,
        in_specs=(both, both, P("bucket", None, None)),
        out_specs=both,
        check_vma=False,
    )
```

```python
import functools

import jax
import jax.numpy as jnp
from jax import lax
from jax.experimental import pallas as pl
from jax.experimental.pallas import tpu as pltpu
from jax.sharding import PartitionSpec as P

CELLS = 16
SWEEPS = 3
CAP = 128
D = 768
RB = 128
NB = D // RB
ROWS = 1024
SLOTS = CELLS * CAP
F32 = jnp.float32
BF16 = jnp.bfloat16
NT = (((1,), (1,)), ((), ()))
TN = (((0,), (0,)), ((), ()))
VMEM = pl.BlockSpec(memory_space=pltpu.VMEM)
ANY = pl.BlockSpec(memory_space=pl.ANY)
HBM = pl.BlockSpec(memory_space=pltpu.HBM)
MESH = pl.DeviceIdType.MESH
DMA = pltpu.SemaphoreType.DMA
PLANE = 16
RING = 8
PAIRS = [(i, j) for i in range(NB) for j in range(i, NB)]
CHUNK = 176
HALF = RING * CHUNK
PACKED = 2 * HALF
TAIL = len(PAIRS) * RB
PIECES = 12
ORDER = (
    (0, 1), (2, 2), (1, 0), (1, 2), (0, 3), (2, 1), (3, 0), (2, 3),
    (1, 1), (0, 2), (3, 3), (2, 0), (1, 3), (3, 2), (3, 1),
)
PIECE = D // PIECES


def params(mib, **kw):
    return pltpu.CompilerParams(vmem_limit_bytes=mib * 2**20, **kw)


def dot(a, b):
    return jnp.dot(a, b, preferred_element_type=F32)


def dot_nt(a, b):
    return lax.dot_general(a, b, NT, preferred_element_type=F32)


def side(parts):
    return jnp.concatenate(parts, axis=1)


def pile(parts):
    return jnp.concatenate(parts, axis=0)


def thirds(x):
    high = x.astype(BF16)
    left = x - high.astype(F32)
    middle = left.astype(BF16)
    return high, middle, (left - middle.astype(F32)).astype(BF16)


def halves(x):
    high = x.astype(BF16)
    return high, (x - high.astype(F32)).astype(BF16)


def scatter_kernel(
    ids_ref, rows_hbm, basis_ref, received_ref, got_counts_ref, got_basis_ref, place_ref,
    buffer, counts, rows_ref,
    send, recv, send_count, recv_count, send_up, send_down, send_across, recv_chain, recv_across, own
):
    bucket, me = lax.axis_index("bucket"), lax.axis_index("replica")
    z, core = bucket // 2, bucket % 2
    origin, chain_core = me // 2, me % 2
    away = lax.rem(z + RING - origin, RING)
    up = lax.rem(z + 1, RING) * 2 + core
    down = lax.rem(z + RING - 1, RING) * 2 + core
    across = z * 2 + (1 - core)
    peers = plane_peers(me)
    load = pltpu.make_async_copy(rows_hbm, rows_ref, own.at[3])
    load.start()

    barrier = pltpu.get_barrier_semaphore()
    for peer in peers:
        pl.semaphore_signal(barrier, inc=1, device_id=(bucket, peer), device_id_type=MESH)
    for other in (up, down, across):
        pl.semaphore_signal(barrier, inc=1, device_id=(other, me), device_id_type=MESH)
    pl.semaphore_wait(barrier, len(peers) + 3)

    def passing(source, index, sends, receives, target):
        span = pl.ds(index * PIECE, PIECE)
        return pltpu.make_async_remote_copy(
            source.at[span], got_basis_ref.at[span], sends.at[index], receives.at[index],
            device_id=(target, me), device_id_type=MESH,
        )

    on_chain = core == chain_core
    first = on_chain & (away == 0)
    later = on_chain & (away > 0)

    whole = pltpu.make_async_copy(basis_ref, got_basis_ref, own.at[2])

    @pl.when(first)
    def _():
        for index in range(PIECES):
            passing(basis_ref, index, send_up, recv_chain, up).start()
            passing(basis_ref, index, send_down, recv_chain, down).start()
            passing(basis_ref, index, send_across, recv_across, across).start()
        whole.start()

    ids = ids_ref[...]
    cells = lax.broadcasted_iota(jnp.int32, (CELLS, ROWS), 0)
    onehot = (ids == cells).astype(F32)
    before = (
        lax.broadcasted_iota(jnp.int32, (ROWS, ROWS), 0)
        < lax.broadcasted_iota(jnp.int32, (ROWS, ROWS), 1)
    ).astype(F32).astype(BF16)
    ranks = dot(onehot.astype(BF16), before)
    slot = jnp.sum(ranks * onehot, axis=0, keepdims=True).astype(jnp.int32)
    place = ids * CAP + slot
    eighth = lax.broadcasted_iota(jnp.int32, (8 * CELLS, ROWS), 0) // 8
    each = jnp.sum((ids == eighth).astype(F32), axis=1, keepdims=True)
    counts[...] = jnp.broadcast_to(each, (8 * CELLS, 128))

    def fill(cell):
        wanted = lax.broadcasted_iota(jnp.int32, (CAP, ROWS), 0) + cell * CAP
        pick = (place == wanted).astype(F32).astype(BF16)
        start = pl.multiple_of(cell * CAP, CAP)
        buffer[pl.ds(start, CAP), :] = dot(pick, rows_ref[...]).astype(BF16)

    load.wait()
    copies = []
    for index, peer in enumerate(peers):
        fill(peer)
        copies.append(exchange(buffer, received_ref, send, recv, index, bucket, me, peer))
        copies[-1].start()
    fill(me)
    for index, peer in enumerate(peers):
        copies.append(pltpu.make_async_remote_copy(
            counts.at[pl.ds(pl.multiple_of(peer * 8, 8), 8)],
            got_counts_ref.at[pl.ds(pl.multiple_of(me * 8, 8), 8)],
            send_count.at[index], recv_count.at[index], device_id=(bucket, peer), device_id_type=MESH,
        ))
        copies[-1].start()
    mine = pl.ds(pl.multiple_of(me * CAP, CAP), CAP)
    mine_counts = pl.ds(pl.multiple_of(me * 8, 8), 8)
    local = [
        pltpu.make_async_copy(buffer.at[mine], received_ref.at[mine], own.at[0]),
        pltpu.make_async_copy(counts.at[mine_counts], got_counts_ref.at[mine_counts], own.at[1]),
    ]
    for copy in local:
        copy.start()
    place_ref[...] = jnp.broadcast_to(place, (128, ROWS)).T

    @pl.when(first)
    def _():
        for index in range(PIECES):
            passing(basis_ref, index, send_up, recv_chain, up).wait_send()
            passing(basis_ref, index, send_down, recv_chain, down).wait_send()
            passing(basis_ref, index, send_across, recv_across, across).wait_send()
        whole.wait()

    @pl.when(later)
    def _():
        upward = away < 4
        downward = away > 5
        for index in range(PIECES):
            passing(got_basis_ref, index, send_up, recv_chain, up).wait_recv()

            @pl.when(upward)
            def _():
                passing(got_basis_ref, index, send_up, recv_chain, up).start()

            @pl.when(downward)
            def _():
                passing(got_basis_ref, index, send_down, recv_chain, down).start()

            passing(got_basis_ref, index, send_across, recv_across, across).start()
        for index in range(PIECES):
            @pl.when(upward)
            def _():
                passing(got_basis_ref, index, send_up, recv_chain, up).wait_send()

            @pl.when(downward)
            def _():
                passing(got_basis_ref, index, send_down, recv_chain, down).wait_send()

            passing(got_basis_ref, index, send_across, recv_across, across).wait_send()

    @pl.when(core != chain_core)
    def _():
        for index in range(PIECES):
            passing(got_basis_ref, index, send_across, recv_across, across).wait_recv()

    for copy in copies + local:
        copy.wait()


def plane_peers(me):
    y, x = me // 4, me % 4
    return [
        lax.rem(y + dy, 4) * 4 + lax.rem(x + dx, 4)
        for dy, dx in ORDER
    ]


def exchange(source, target, send, recv, index, bucket, me, peer):
    return pltpu.make_async_remote_copy(
        source.at[pl.ds(pl.multiple_of(peer * CAP, CAP), CAP)],
        target.at[pl.ds(pl.multiple_of(me * CAP, CAP), CAP)],
        send.at[index], recv.at[index], device_id=(bucket, peer), device_id_type=MESH,
    )


def giveback_kernel(received_ref, w_ref, shift_ref, returned_ref, rotated, send, recv, own):
    bucket, me = lax.axis_index("bucket"), lax.axis_index("replica")
    peers = plane_peers(me)
    barrier = pltpu.get_barrier_semaphore()
    for peer in peers:
        pl.semaphore_signal(barrier, inc=1, device_id=(bucket, peer), device_id_type=MESH)
    pl.semaphore_wait(barrier, len(peers))

    def block(peer):
        return pl.ds(pl.multiple_of(peer * CAP, CAP), CAP)

    copies = []
    order = peers + [me]
    for index in range(0, PLANE, 2):
        pair = order[index : index + 2]
        product = dot_nt(pile([received_ref[block(peer), :] for peer in pair]), w_ref[...])
        values = (product - shift_ref[0:1, :]).astype(BF16)
        for half, peer in enumerate(pair):
            rotated[block(peer), :] = values[half * CAP : half * CAP + CAP, :]
            if index + half < PLANE - 1:
                copies.append(
                    exchange(rotated, returned_ref, send, recv, index + half, bucket, me, peer)
                )
            else:
                copies.append(
                    pltpu.make_async_copy(rotated.at[block(me)], returned_ref.at[block(me)], own.at[0])
                )
            copies[-1].start()
    for copy in copies:
        copy.wait()


def moments_kernel(received_ref, counts_ref, out_ref):
    place = 0
    for block in range(NB):
        rest = slice(block * RB, D)
        square = lax.dot_general(
            received_ref[:, block * RB : block * RB + RB], received_ref[:, rest], TN,
            preferred_element_type=F32,
        )
        for other in range(NB - block):
            out_ref[place : place + RB, :] = square[:, other * RB : other * RB + RB]
            place += RB
    total = dot(jnp.ones((8, SLOTS), BF16), received_ref[...])
    out_ref[TAIL:PACKED, :] = jnp.zeros((PACKED - TAIL, RB), F32)
    for block in range(NB):
        out_ref[TAIL + block : TAIL + block + 1, :] = total[0:1, block * RB : block * RB + RB]
    count = jnp.sum(counts_ref[...].reshape(CELLS, 8, 128)[:, 0, :], axis=0, keepdims=True)
    out_ref[TAIL + NB : TAIL + NB + 1, :] = count


def reduce_kernel(
    part_ref, out_ref, full, arrived, mine, slots, send_half, recv_half, send_part, recv_part,
    send_all, recv_all, send_across, recv_across
):
    bucket, me = lax.axis_index("bucket"), lax.axis_index("replica")
    z, core = bucket // 2, bucket % 2
    across = (z * 2 + (1 - core), me)
    ring = [(lax.rem(z + step, RING) * 2 + core, me) for step in range(RING)]
    barrier = pltpu.get_barrier_semaphore()
    for other in [across] + ring[1:]:
        pl.semaphore_signal(barrier, inc=1, device_id=other, device_id_type=MESH)
    pl.semaphore_wait(barrier, RING)

    def rows_of(chunk):
        return pl.ds(pl.multiple_of(chunk * CHUNK, 8), CHUNK)

    order = [1, 7, 2, 6, 3, 5, 4]
    halves_out = {}
    for step in order + [0]:
        chunk = lax.rem(z + step, RING)
        halves_out[step] = pltpu.make_async_remote_copy(
            part_ref.at[rows_of((1 - core) * RING + chunk)], arrived.at[rows_of(chunk)],
            send_half.at[step], recv_half.at[step], device_id=across, device_id_type=MESH,
        )
        halves_out[step].start()

    def add_pair(step):
        chunk = lax.rem(z + step, RING)
        halves_out[step].wait_recv()
        mine[rows_of(chunk), :] = part_ref[rows_of(core * RING + chunk), :] + arrived[rows_of(chunk), :]

    parts = []
    for step in order:
        add_pair(step)
        parts.append(pltpu.make_async_remote_copy(
            mine.at[rows_of(lax.rem(z + step, RING))], slots.at[step],
            send_part.at[step], recv_part.at[step], device_id=ring[step], device_id_type=MESH,
        ))
        parts[-1].start()
    add_pair(0)
    total = mine[rows_of(z), :]
    for step, copy in zip(order, parts):
        copy.wait_recv()
        total = total + slots[step]

    def chunk_of(where):
        return pl.ds(pl.multiple_of((core * RING + where) * CHUNK, 8), CHUNK)

    full[chunk_of(z), :] = total
    spread = [
        pltpu.make_async_remote_copy(
            full.at[chunk_of(z)], full.at[chunk_of(z)], send_all.at[step], recv_all.at[step],
            device_id=ring[step], device_id_type=MESH,
        )
        for step in order
    ]
    for copy in spread:
        copy.start()

    def forward(step):
        where = chunk_of(lax.rem(z + RING - step, RING))
        return pltpu.make_async_remote_copy(
            full.at[where], full.at[where], send_across.at[step], recv_across.at[step],
            device_id=across, device_id_type=MESH,
        )

    forward(0).start()
    for step, copy in sorted(zip(order, spread), key=lambda item: min(item[0], RING - item[0])):
        copy.wait_recv()
        forward(step).start()
    for step in range(RING):
        forward(step).wait()
    for copy in parts + spread + list(halves_out.values()):
        copy.wait_send()
    out_ref[...] = full[...]


def factor(a_ref, m_ref, columns):
    n = RB // 8
    shape = (8, RB)
    sub = lax.broadcasted_iota(jnp.int32, shape, 0)
    lane = lax.broadcasted_iota(jnp.int32, shape, 1)
    x = [a_ref[8 * r : 8 * r + 8, :] for r in range(n)]

    def wide(v):
        return jnp.broadcast_to(v, shape)

    def assemble(v):
        out = v[0]
        for j in range(1, 8):
            out = jnp.where(sub == j, v[j], out)
        return out

    for b in range(n):
        near = min(b + 2, n)
        inside = (lane >= 8 * b) & (lane < 8 * b + 8)
        col = {
            r: [wide(x[r][:, 8 * b + j : 8 * b + j + 1]) for j in range(8)] for r in range(b, near)
        }
        base = 64 * (b % 2)
        for j in range(8):
            columns[base + 8 * j : base + 8 * j + 8, :] = col[b][j]
        s = [
            [columns[pl.ds(base + 8 * j + i, 8, stride=0), :] if i >= j else None for j in range(8)]
            for i in range(8)
        ]
        t = [[None] * 8 for _ in range(8)]
        inverse = [None] * 8
        for j in range(0, 8, 2):
            p, q, w = s[j][j], s[j + 1][j], s[j + 1][j + 1]
            inverse[j] = 1.0 / p
            t[j + 1][j] = q * inverse[j]
            both = 1.0 / (p * w - q * q)
            inverse[j + 1] = p * both
            for i in range(j + 2, 8):
                t[i][j] = s[i][j] * inverse[j]
                t[i][j + 1] = (s[i][j + 1] * p - s[i][j] * q) * both
            for k in range(j + 2, 8):
                g0 = (s[k][j] * w - s[k][j + 1] * q) * both
                for i in range(k, 8):
                    s[i][k] = s[i][k] - g0 * s[i][j] - t[k][j + 1] * s[i][j + 1]
            s[j + 1][j + 1] = w - t[j + 1][j] * q
        low = {}
        for r in range(b, near):
            c = list(col[r])
            low[r] = []
            for j in range(8):
                for i in range(j + 1, 8):
                    c[i] = c[i] - c[j] * t[i][j]
                low[r].append(c[j] * inverse[j])
        panel = jnp.where(inside, (lane == sub + 8 * b).astype(F32), x[b])
        rows = []
        for j in range(8):
            rows.append(wide(panel[j : j + 1, :]))
            if j < 7:
                panel = panel - jnp.where(sub > j, low[b][j], 0.0) * rows[j]
        pivots = assemble([s[j][j] for j in range(8)])
        x[b] = jnp.where(lane < 8 * b + 8, panel * lax.rsqrt(pivots), 0.0)
        for r in range(b + 1, near):
            even, odd = low[r][0] * rows[0], low[r][1] * rows[1]
            for j in range(2, 8, 2):
                even = even + low[r][j] * rows[j]
                odd = odd + low[r][j + 1] * rows[j + 1]
            x[r] = jnp.where(inside, 0.0, x[r]) - (even + odd)
        if near < n:
            g = [rows[j] * inverse[j] for j in range(8)]
            for j in range(7, 0, -1):
                for i in range(j):
                    g[i] = g[i] - t[j][i] * g[j]
            above = [jnp.zeros((8 * b, RB), F32)] if b else []
            below = [jnp.zeros((RB - 8 * b - 8, RB), F32)]
            g_high, g_low = halves(jnp.concatenate(above + [assemble(g)] + below, axis=0))
            x_high, x_low = halves(jnp.concatenate(x[near:], axis=0))
            two = dot(x_high, side([g_high, g_low]))
            change = two[:, :RB] + two[:, RB:] + dot(x_low, g_high)
            for r in range(near, n):
                first = 8 * (r - near)
                x[r] = jnp.where(inside, 0.0, x[r]) - change[first : first + 8, :]
    for r in range(n):
        m_ref[8 * r : 8 * r + 8, :] = x[r]


def sweeps_kernel(
    reduced_ref, start_ref, w_high, shift_ref, c_high, c_low, y, y_high, y_low, w_low, gram, inverse, spread_columns
):
    count = reduced_ref[TAIL + NB : TAIL + NB + 1, :]
    divisor = jnp.maximum(count, 1.0)
    mean = jnp.concatenate(
        [reduced_ref[TAIL + block : TAIL + block + 1, :] / divisor for block in range(NB)], axis=1
    )
    m1, m2, m3 = thirds(jnp.broadcast_to(mean, (16, D)))
    row = lax.broadcasted_iota(jnp.int32, (16, D), 0)
    nothing = jnp.zeros((16, D), F32)
    m1, m2, m3 = m1.astype(F32), m2.astype(F32), m3.astype(F32)

    def stack(parts):
        out = nothing
        for index, part in enumerate(parts):
            out = jnp.where(row == index, part, out)
        return out.astype(BF16)

    mean_left = stack([m1, m1, m2, m1, m3, m2])
    mean_right = stack([m1, m2, m1, m3, m1, m2])
    for block in range(NB):
        span = slice(block * RB, block * RB + RB)
        outer = lax.dot_general(
            mean_left[:, span], mean_right, TN, preferred_element_type=F32,
        )
        for other in range(NB):
            columns = slice(other * RB, other * RB + RB)
            place = PAIRS.index((min(block, other), max(block, other))) * RB
            piece = reduced_ref[place : place + RB, :]
            if other < block:
                piece = piece.T
            high, low = halves(piece / divisor - outer[:, columns])
            c_high[span, columns] = high
            c_low[span, columns] = low
        high, low = halves(start_ref[:, span].T)
        w_high[span, :] = high
        w_low[span, :] = low

    def sweep(step, carry):
        for block in range(D // 256):
            span = slice(block * 256, block * 256 + 256)
            high, low = w_high[span, :], w_low[span, :]
            image = dot(side([high, high, low]), pile([c_high[...], c_low[...], c_high[...]]))
            y[span, :] = image
            high, low = halves(image)
            y_high[span, :] = high
            y_low[span, :] = low
            if block == 0:
                high, low = high[:RB, :], low[:RB, :]
                gram[...] = dot_nt(side([high, high, low]), side([high, low, high]))

        last = step == SWEEPS - 1

        def block_step(block, inner):
            factor(gram, inverse, spread_columns)

            def finish(done, exact):
                own = slice(RB * done, RB * done + RB)
                high, low = y_high[own, :], y_low[own, :]
                i_high, i_low = halves(inverse[...])
                if exact:
                    kept = dot(side([i_high, i_high, i_low]), pile([high, low, high]))
                else:
                    kept = dot(side([i_high, i_high]), pile([high, low]))
                u_h, u_l = halves(kept)
                w_high[own, :] = u_h
                w_low[own, :] = u_l
                if done == NB - 1:
                    return
                rest = slice(RB * (done + 1), D)
                if exact:
                    r_h, r_l = y_high[rest, :], y_low[rest, :]
                    l_h, l_l = halves(dot_nt(side([r_h, r_h, r_l]), side([u_h, u_l, u_h])))
                    change = dot(side([l_h, l_h, l_l]), pile([u_h, u_l, u_h]))
                else:
                    l_h = dot_nt(y_high[rest, :], u_h).astype(BF16)
                    change = dot(side([l_h, l_h]), pile([u_h, u_l]))
                left = y[rest, :] - change
                high, low = halves(left)
                y[rest, :] = left
                y_high[rest, :] = high
                y_low[rest, :] = low
                high, low = high[:RB, :], low[:RB, :]
                if exact:
                    gram[...] = dot_nt(side([high, high, low]), side([high, low, high]))
                else:
                    gram[...] = dot_nt(high, high)

            for done in range(NB):
                pl.when((block == done) & jnp.logical_not(last))(
                    functools.partial(finish, done, False)
                )
                pl.when((block == done) & last)(functools.partial(finish, done, True))
            return inner

        return lax.fori_loop(0, NB, block_step, carry)

    lax.fori_loop(0, SWEEPS, sweep, 0)
    shifts = dot_nt(stack([m1, m2, m3]), w_high[...])
    shift_ref[...] = jnp.broadcast_to(shifts[0:1, :] + shifts[1:2, :] + shifts[2:3, :], (8, D))


def collect_kernel(returned_ref, place_ref, out_ref):
    def step(index, carry):
        span = pl.ds(pl.multiple_of(index * 256, 256), 256)
        place = place_ref[span, :]
        lane = lax.broadcasted_iota(jnp.int32, (256, CAP), 1)
        pick = jnp.concatenate(
            [(place == lane + cell * CAP).astype(F32).astype(BF16) for cell in range(CELLS)], axis=1
        )
        out_ref[span, :] = dot(pick, returned_ref[...]).astype(BF16)
        return carry

    lax.fori_loop(0, ROWS // 256, step, 0)


def sweeps(reduced, start):
    return pl.pallas_call(
        sweeps_kernel,
        out_shape=[jax.ShapeDtypeStruct((D, D), BF16), jax.ShapeDtypeStruct((8, D), F32)],
        in_specs=[VMEM, VMEM],
        out_specs=[VMEM, VMEM],
        scratch_shapes=[
            pltpu.VMEM((D, D), BF16),
            pltpu.VMEM((D, D), BF16),
            pltpu.VMEM((D, D), F32),
            pltpu.VMEM((D, D), BF16),
            pltpu.VMEM((D, D), BF16),
            pltpu.VMEM((D, D), BF16),
            pltpu.VMEM((RB, RB), F32),
            pltpu.VMEM((RB, RB), F32),
            pltpu.VMEM((RB + 8, RB), F32),
        ],
        compiler_params=params(48),
        name="sweeps",
    )(reduced, start)


def remote(identity):
    return params(40, collective_id=identity, has_side_effects=True)


def body(rows, cell_ids, start_basis):
    received, got_counts, basis, place = pl.pallas_call(
        scatter_kernel,
        out_shape=[
            jax.ShapeDtypeStruct((SLOTS, D), BF16),
            jax.ShapeDtypeStruct((8 * CELLS, 128), F32),
            jax.ShapeDtypeStruct((D, D), F32),
            jax.ShapeDtypeStruct((ROWS, 128), jnp.int32),
        ],
        in_specs=[VMEM, HBM, HBM],
        out_specs=[ANY] * 3 + [VMEM],
        scratch_shapes=[
            pltpu.VMEM((SLOTS, D), BF16),
            pltpu.VMEM((8 * CELLS, 128), F32),
            pltpu.VMEM((ROWS, D), BF16),
        ]
        + [DMA((PLANE - 1,))] * 4 + [DMA((PIECES,))] * 5 + [DMA((4,))],
        compiler_params=remote(1),
        name="scatter",
    )(cell_ids.reshape(1, ROWS), rows, start_basis[0])
    partial = pl.pallas_call(
        moments_kernel,
        out_shape=jax.ShapeDtypeStruct((PACKED, RB), F32),
        in_specs=[VMEM, VMEM],
        out_specs=VMEM,
        compiler_params=params(40),
        name="moments",
    )(received, got_counts)
    reduced = pl.pallas_call(
        reduce_kernel,
        out_shape=jax.ShapeDtypeStruct((PACKED, RB), F32),
        in_specs=[VMEM],
        out_specs=VMEM,
        scratch_shapes=[
            pltpu.VMEM((PACKED, RB), F32),
            pltpu.VMEM((HALF, RB), F32),
            pltpu.VMEM((HALF, RB), F32),
            pltpu.VMEM((RING, CHUNK, RB), F32),
        ] + [DMA((RING,))] * 8,
        compiler_params=remote(2),
        name="reduce",
    )(partial)
    rotation, shift = sweeps(reduced, basis)
    returned = pl.pallas_call(
        giveback_kernel,
        out_shape=jax.ShapeDtypeStruct((SLOTS, D), BF16),
        in_specs=[VMEM] * 3,
        out_specs=ANY,
        scratch_shapes=[pltpu.VMEM((SLOTS, D), BF16)] + [DMA((PLANE - 1,))] * 2 + [DMA((1,))],
        compiler_params=remote(3),
        name="giveback",
    )(received, rotation, shift)
    return pl.pallas_call(
        collect_kernel,
        out_shape=jax.ShapeDtypeStruct((ROWS, D), BF16),
        in_specs=[VMEM] * 2,
        out_specs=VMEM,
        compiler_params=params(40),
        name="collect",
    )(returned, place)


def solution(mesh):
    both = P(("bucket", "replica"), None)
    return jax.shard_map(
        body,
        mesh=mesh,
        in_specs=(both, both, P("bucket", None, None)),
        out_specs=both,
        check_vma=False,
    )
```
